128 devices in a mesh: segment: 16 (over x, y_lo, core), tensor: 8 (over y_hi, z).
Axes of the slice: x: 4, y: 4 (y_hi: 2, y_lo: 2; y = y_hi * 2 + y_lo), z: 4, core: 2. Of those that a mesh axis runs over, the one named last changes fastest.
Arguments:
- hidden: bfloat16 [16, 2, 384, 8192], P('segment', None, None, 'tensor'), may hold values from -6 to 6
- norm_gain: bfloat16 [16, 8192], P('segment'), may hold values from 0.099609375 to 1.8984375
- query_weight: bfloat16 [16, 8192, 4096], P('segment', None, 'tensor'), may hold values from -0.0625 to 0.0625
- query_bias: bfloat16 [16, 4096], P('segment', 'tensor'), may hold values from -4 to 4
- key_value_weight: bfloat16 [16, 2, 8192, 512], P('segment', None, None, 'tensor'), may hold values from -0.0625 to 0.0625
- key_value_bias: bfloat16 [16, 2, 512], P('segment', None, 'tensor'), may hold values from -4 to 4
- output_weight: bfloat16 [16, 4096, 8192], P('segment', 'tensor'), may hold values from -0.09375 to 0.09375
- resident_cache: bfloat16 [16, 2, 2, 1024, 512], P('segment', None, None, None, 'tensor'), may hold values from -210 to 210
- resident_length: int32 [16, 2], P('segment'), may hold values from 256 to 1024, as said below
- plan: int32 [16, 2], P('segment'), may hold values from 0 to 1, each once within a row
- page_owner: int32 [16, 6], P('segment'), may hold values from 0 to 15, as said below
Outputs:
- next_hidden: bfloat16 [16, 2, 384, 8192], P('segment', None, None, 'tensor')
- shipped_pages: bfloat16 [16, 16, 2, 128, 512], P('segment', None, None, None, 'tensor')
The draws below stay inside these ranges and needn't reach their ends.
Inputs may be any that keep to these rules, and one draw needn't show every extreme that they name: `resident_length`: some block has exactly 1024 earlier tokens. `page_owner`: within one section's row all owners differ; one owner appears in every section's row. `plan`: each section's row names every block once.
All inputs are finite; a program needn't handle non-finite values.
Results may differ from the reference program's by a relative error of at most 0.015.
Values may be sent and summed in bfloat16 or wider, within the bound.
No kernel may reach another device: no remote copies, remote signals or barrier semaphores. Data moves between devices by JAX's collectives and lax.ppermute only.
A program may use at most 128 MiB of HBM per device.

```python
import math
import jax
import jax.numpy as jnp
from jax import lax

D = 8192
HEADS = 32
KV_HEADS = 4
HEAD_DIM = 128
BLOCKS = 2
ROWS = 384
RES = 1024
PAGE = 128
PAGES_DEV = 6
N_SEGMENT = 16
N_TENSOR = 8


def draw_resident_cache(key, part):
    key = jax.random.fold_in(key, 11)
    first_key, second_key, third_key = jax.random.split(key, 3)
    shape_full = (N_SEGMENT, BLOCKS, RES, KV_HEADS * HEAD_DIM)
    key_part = jax.random.truncated_normal(first_key, -4.0, 4.0, shape_full, jnp.float32)
    centre = jax.random.uniform(second_key, (N_SEGMENT, BLOCKS, 1, KV_HEADS * HEAD_DIM), jnp.float32, -1.5, 1.5)
    value_part = centre + jax.random.truncated_normal(third_key, -4.0, 4.0, shape_full, jnp.float32)
    return jnp.stack([key_part, value_part], axis=2).astype(jnp.bfloat16)


def draw_resident_length(key, part):
    key = jax.random.fold_in(key, 12)
    first_key, second_key = jax.random.split(key)
    lengths = jax.random.randint(first_key, (N_SEGMENT, BLOCKS), RES // 4, RES + 1)
    chosen = jax.random.randint(second_key, (), 0, N_SEGMENT * BLOCKS)
    flat_index = jnp.arange(N_SEGMENT * BLOCKS).reshape(N_SEGMENT, BLOCKS)
    return jnp.where(flat_index == chosen, RES, lengths).astype(jnp.int32)


def draw_page_owner(key, part):
    key = jax.random.fold_in(key, 13)
    first_key, second_key, third_key = jax.random.split(key, 3)
    hottest = jax.random.randint(first_key, (), 0, N_SEGMENT)
    shuffled = jax.vmap(lambda single: jax.random.permutation(single, N_SEGMENT - 1))(jax.random.split(second_key, N_SEGMENT))
    others = (hottest + 1 + shuffled[:, :PAGES_DEV - 1]) % N_SEGMENT
    complete = jnp.concatenate([jnp.full((N_SEGMENT, 1), hottest), others], axis=1)
    ordering = jax.vmap(lambda single: jax.random.permutation(single, PAGES_DEV))(jax.random.split(third_key, N_SEGMENT))
    return jnp.take_along_axis(complete, ordering, axis=1).astype(jnp.int32)


def steps_of(own_key, extent, cuts, least, high):
    def one(dim, parts):
        draws = jax.random.uniform(jax.random.fold_in(jax.random.fold_in(own_key, 6), dim), (parts,), jnp.float32, least / len(cuts), high / len(cuts))
        return jnp.repeat(jnp.exp(draws), extent[dim] // parts).reshape((-1,) + (1,) * (len(extent) - dim - 1))

    loudness = one(*cuts[0])
    for cut in cuts[1:]:
        loudness = loudness * one(*cut)
    return loudness


def gaussian(stream_key, extent, spread, limit, cuts=(), kind=jnp.bfloat16):
    level = steps_of(stream_key, extent, cuts, -0.22, 0.18) if cuts else 1.0
    values = jax.random.normal(stream_key, extent, jnp.float32) * spread * level
    return jnp.minimum(jnp.maximum(values, -limit), limit).astype(kind)


def setup_inputs(seed: int = 0) -> dict:
    key_list = jax.random.split(jax.random.key(seed), 12)
    hidden = gaussian(key_list[0], (N_SEGMENT, BLOCKS, ROWS, D), 1.0, 6.0, ((0, 16), (3, 8)))
    norm_gain = jnp.clip(1.0 + 0.18 * jax.random.normal(key_list[1], (N_SEGMENT, D), jnp.float32), 0.099609375, 1.8984375).astype(jnp.bfloat16)
    query_weight = gaussian(key_list[2], (N_SEGMENT, D, HEADS * HEAD_DIM), D ** -0.5, 0.0625, ((0, 16), (2, 8)))
    query_bias = gaussian(key_list[3], (N_SEGMENT, HEADS * HEAD_DIM), 1.0, 4.0, ((0, 16), (1, 8)))
    key_value_weight = gaussian(key_list[4], (N_SEGMENT, 2, D, KV_HEADS * HEAD_DIM), D ** -0.5, 0.0625, ((0, 16), (3, 8)))
    key_value_bias = gaussian(key_list[5], (N_SEGMENT, 2, KV_HEADS * HEAD_DIM), 1.0, 4.0, ((0, 16), (2, 8)))
    output_weight = gaussian(key_list[6], (N_SEGMENT, HEADS * HEAD_DIM, D), (HEADS * HEAD_DIM) ** -0.5, 0.09375, ((0, 16), (1, 8)))
    resident_cache = draw_resident_cache(jax.random.fold_in(key_list[11], 71), 0)
    resident_length = draw_resident_length(jax.random.fold_in(key_list[11], 71), 0)
    plan = jax.vmap(lambda own: jax.random.permutation(own, BLOCKS))(jax.random.split(key_list[9], N_SEGMENT)).reshape((N_SEGMENT, BLOCKS)).astype(jnp.int32)
    page_owner = draw_page_owner(jax.random.fold_in(key_list[11], 71), 0)
    return dict(hidden=hidden, norm_gain=norm_gain, query_weight=query_weight, query_bias=query_bias, key_value_weight=key_value_weight, key_value_bias=key_value_bias, output_weight=output_weight, resident_cache=resident_cache, resident_length=resident_length, plan=plan, page_owner=page_owner)


def rope_tables(first_place, row_count):
    half_dim = HEAD_DIM // 2
    position = first_place.astype(jnp.float32) + jnp.arange(row_count, dtype=jnp.float32)
    frequency = jnp.exp(jnp.arange(half_dim, dtype=jnp.float32) * (-2.0 * math.log(1000000.0) / HEAD_DIM))
    angles = position[:, None] * frequency[None, :]
    return (jnp.cos(angles)[:, None, :], jnp.sin(angles)[:, None, :])

def rotate(vectors, cosine, sine_table):
    half_dim = vectors.shape[-1] // 2
    first_half = vectors[..., :half_dim]
    second_half = vectors[..., half_dim:]
    return jnp.concatenate([first_half * cosine - second_half * sine_table, second_half * cosine + first_half * sine_table], axis=-1)

def attend(queries, all_keys, all_values, key_length, row_count):
    key_count = all_keys.shape[0]
    resident_count = key_count - row_count
    key_index = jnp.arange(key_count)[None, :]
    query_index = jnp.arange(row_count)[:, None]
    allowed = jnp.where(key_index < resident_count, key_index < key_length, key_index - resident_count <= query_index)
    scores = jnp.einsum('rkgd,tkd->kgrt', queries.astype(jnp.float32), all_keys.astype(jnp.float32)) * (1.0 / math.sqrt(HEAD_DIM))
    scores = jnp.where(allowed, scores, -jnp.inf)
    row_max = lax.optimization_barrier(jnp.max(scores, axis=-1, keepdims=True))
    weights = jnp.exp(scores - row_max)
    probabilities = (weights / lax.optimization_barrier(jnp.sum(weights, axis=-1, keepdims=True))).astype(jnp.bfloat16)
    combined = jnp.einsum('kgrt,tkd->rkgd', probabilities.astype(jnp.float32), all_values.astype(jnp.float32))
    return combined.reshape(row_count, -1).astype(jnp.bfloat16)

def section(hidden, norm_gain, query_weight, query_bias, key_value_weight, key_value_bias, output_weight, resident_cache, resident_length):
    widened = hidden.astype(jnp.float32)
    inverse_rms = lax.rsqrt(lax.optimization_barrier(jnp.mean(widened * widened, axis=-1, keepdims=True)) + 1e-06)
    normalized = (widened * inverse_rms * norm_gain.astype(jnp.float32)).astype(jnp.bfloat16)
    group_size = HEADS // KV_HEADS
    results = []
    page_list = []
    for block in range(BLOCKS):
        block_rows = normalized[block]
        cosine, sine_table = rope_tables(resident_length[block], ROWS)
        queries = jnp.dot(block_rows, query_weight, preferred_element_type=jnp.float32) + query_bias.astype(jnp.float32)
        queries = rotate(queries.reshape(ROWS, HEADS, HEAD_DIM), cosine, sine_table).astype(jnp.bfloat16)
        queries = queries.reshape(ROWS, KV_HEADS, group_size, HEAD_DIM)
        fresh_keys = jnp.dot(block_rows, key_value_weight[0], preferred_element_type=jnp.float32) + key_value_bias[0].astype(jnp.float32)
        fresh_keys = rotate(fresh_keys.reshape(ROWS, KV_HEADS, HEAD_DIM), cosine, sine_table).astype(jnp.bfloat16)
        fresh_values = jnp.dot(block_rows, key_value_weight[1], preferred_element_type=jnp.float32) + key_value_bias[1].astype(jnp.float32)
        fresh_values = fresh_values.astype(jnp.bfloat16).reshape(ROWS, KV_HEADS, HEAD_DIM)
        all_keys = jnp.concatenate([resident_cache[block, 0].reshape(RES, KV_HEADS, HEAD_DIM), fresh_keys], axis=0)
        all_values = jnp.concatenate([resident_cache[block, 1].reshape(RES, KV_HEADS, HEAD_DIM), fresh_values], axis=0)
        attended = attend(queries, all_keys, all_values, resident_length[block], ROWS)
        head_groups = attended.reshape(ROWS, N_TENSOR, -1).astype(jnp.float32)
        partials = jnp.einsum('rtk,tkd->trd', head_groups, output_weight.reshape(N_TENSOR, -1, D).astype(jnp.float32))
        partials = lax.optimization_barrier(partials.astype(jnp.bfloat16)).astype(jnp.float32)
        results.append((widened[block] + lax.optimization_barrier(jnp.sum(partials, axis=0))).astype(jnp.bfloat16))
        page_list.append(jnp.stack([fresh_keys.reshape(ROWS // PAGE, PAGE, -1), fresh_values.reshape(ROWS // PAGE, PAGE, -1)], axis=1))
    return (jnp.stack(results), jnp.concatenate(page_list, axis=0))

def reference(hidden, norm_gain, query_weight, query_bias, key_value_weight, key_value_bias, output_weight, resident_cache, resident_length, plan, page_owner):
    layer_out, made_pages = lax.map(lambda operands: section(*operands), (hidden, norm_gain, query_weight, query_bias, key_value_weight, key_value_bias, output_weight, resident_cache, resident_length))
    taken = jnp.take_along_axis(layer_out, plan[:, :, None, None], axis=1)
    next_hidden = jnp.roll(taken, 1, axis=0)
    owner_hits = (page_owner[:, :, None] == jnp.arange(N_SEGMENT, dtype=jnp.int32)[None, None, :]).astype(jnp.float32)
    flat_pages = made_pages.reshape(N_SEGMENT, PAGES_DEV, -1).astype(jnp.float32)
    shipped_pages = jnp.einsum('spo,spx->osx', owner_hits, flat_pages).reshape(N_SEGMENT, N_SEGMENT, 2, PAGE, -1).astype(jnp.bfloat16)
    return (next_hidden, shipped_pages)
```

```python
import functools
import math

import jax
import jax.numpy as jnp
from jax import lax
from jax.experimental import pallas as pl
from jax.experimental.pallas import tpu as pltpu
from jax.sharding import PartitionSpec as P

HEAVY = pl.CostEstimate(flops=0, bytes_accessed=100_000_000, transcendentals=0)
HEAD_DIM = 128
LINK, HERE = "link", 0
LOWER, LENGTH = 8, 9
HALF = HEAD_DIM // 2
PAGE = 128
EPSILON = 1e-06
NZ = 4
TILE = 128
BF = jnp.bfloat16
F32 = jnp.float32

UP = [(y * NZ + z, y * NZ + (z + 1) % NZ) for y in range(2) for z in range(NZ)]
DOWN = [(y * NZ + z, y * NZ + (z - 1) % NZ) for y in range(2) for z in range(NZ)]
ACROSS = [(y * NZ + z, (1 - y) * NZ + z) for y in range(2) for z in range(NZ)]
MATE = [(i, i ^ 1) for i in range(2 * NZ)]

ANY = pl.BlockSpec(memory_space=pl.ANY)


def up(a):
    return lax.ppermute(a, "tensor", UP)


def down(a):
    return lax.ppermute(a, "tensor", DOWN)


def across(a):
    return lax.ppermute(a, "tensor", ACROSS)


def whole(shape):
    return pl.BlockSpec(shape, lambda *_: (0,) * len(shape))


def params(grid_dims=1, mebibytes=16):
    return pltpu.CompilerParams(
        vmem_limit_bytes=mebibytes * 1024 * 1024, dimension_semantics=("arbitrary",) * grid_dims
    )


def hbm(a):
    return pltpu.with_memory_space_constraint(a, pltpu.HBM)


def vmem(a):
    return pltpu.with_memory_space_constraint(a, pltpu.VMEM)


IN_VMEM = pl.BlockSpec(memory_space=pltpu.VMEM)
SMEM = pl.BlockSpec(memory_space=pltpu.SMEM)


def waits_on(waits):
    return [ANY] * len(waits)


def parked(shape, index=None):
    index = (0,) * len(shape) if index is None else index
    return pl.BlockSpec(shape, lambda *_: index, pipeline_mode=pl.Buffered(1))


def product_cost(rows, width, columns, count):
    return pl.CostEstimate(
        flops=2 * rows * width * columns * count,
        bytes_accessed=2 * width * (rows + columns) * count + 8 * rows * columns,
        transcendentals=0,
    )


NT = (((1,), (1,)), ((), ()))


def fold(squared):
    total = squared[:, :HEAD_DIM]
    for start in range(HEAD_DIM, squared.shape[1], HEAD_DIM):
        total = total + squared[:, start : start + HEAD_DIM]
    return total


def add_products(spots, shards, sources, gain, wq, wkv, total, waits=(), only=None):
    count = len(shards)
    blocks, rows, width = shards[0].shape
    place = (0, 0, 0)
    if only is not None:
        blocks, place = 1, (only, 0, 0)
    cols = wq.shape[1]
    fresh_cols = wkv.shape[0]
    first = total is None

    def pick(spot_ref, step):
        chosen = spot_ref[sources[0]]
        for j in range(1, count):
            chosen = jnp.where(step == j, spot_ref[sources[j]], chosen)
        return chosen

    ins = list(shards) + [hbm(gain), hbm(wq), hbm(wkv)]
    ins += ([] if first else [hbm(t) for t in total]) + list(waits)

    def kernel(src_ref, *refs):
        g_ref, wq_ref, wkv_ref = refs[count : count + 3]
        before, after = refs[count + 3 : count + 6], refs[-3:]
        for j in range(count):

            @pl.when(pl.program_id(0) == j)
            def _(j=j):
                x = refs[j][...].reshape(blocks * rows, width).astype(F32)
                scaled = (x * g_ref[...]).astype(BF)
                more = (
                    jnp.dot(scaled, wq_ref[...], preferred_element_type=F32),
                    lax.dot_general(scaled, wkv_ref[...], NT, preferred_element_type=F32),
                    fold(x * x),
                )
                for old, new, term in zip(after if j else before, after, more):
                    term = term.reshape(new.shape)
                    new[...] = term if j == 0 and first else old[...] + term

    shapes = [(blocks, rows, cols), (blocks, rows, fresh_cols), (blocks, rows, HEAD_DIM)]
    in_specs = [parked((blocks, rows, width), place)] * count + [
        pl.BlockSpec((1, width), lambda j, s: (0, pick(s, j))),
        pl.BlockSpec((width, cols), lambda j, s: (pick(s, j), 0)),
        pl.BlockSpec((fresh_cols, width), lambda j, s: (0, pick(s, j))),
    ]
    in_specs += [] if first else [parked(shape, place) for shape in shapes]
    in_specs += waits_on(waits)
    return pl.pallas_call(
        kernel,
        grid_spec=pltpu.PrefetchScalarGridSpec(
            num_scalar_prefetch=1,
            grid=(count,),
            in_specs=in_specs,
            out_specs=[parked(shape) for shape in shapes],
        ),
        out_shape=[pltpu.HBM(shape, F32) for shape in shapes],
        compiler_params=params(1, 32),
        cost_estimate=product_cost(blocks * rows, width, cols + fresh_cols, count),
        name="add_products",
    )(spots, *ins)


def finish_products(spots, block, pieces, source, gain, wq, wkv, total, qb, kvb, cosine, sine, waits=()):
    width = pieces[0].shape[1]
    sizes = [p.shape[0] for p in pieces]
    rows = sum(sizes)
    cols = wq.shape[1]
    fresh_cols = wkv.shape[0]
    half = fresh_cols // 2
    count = len(pieces)
    model = wq.shape[0]

    def kernel(src_ref, *refs):
        g_ref, wq_ref, wkv_ref, q_in, kv_in, sq_in, qb_ref, kvb_ref, cos_ref, sin_ref = refs[
            count : count + 10
        ]
        q_ref, kv_ref, send_ref, x_ref = refs[-4:]
        start = 0
        for piece, size in zip(refs[:count], sizes):
            x_ref[start : start + size] = piece[...]
            start += size
        x = x_ref[...].astype(F32)
        squares = jnp.sum(sq_in[...] + fold(x * x), axis=-1, keepdims=True)
        inverse = lax.rsqrt(squares / model + EPSILON)
        x_ref[...] = (x * g_ref[...]).astype(BF)
        scaled = x_ref[...]
        kv = kv_in[...] + lax.dot_general(scaled, wkv_ref[...], NT, preferred_element_type=F32)
        kv = (kv * inverse + kvb_ref[...]).T.reshape(2, half, rows)
        kv_ref[...] = kv
        send_ref[...] = kv.astype(BF)
        cos, sin = cos_ref[...], sin_ref[...]
        cos = jnp.concatenate([cos, cos], axis=0).T
        sin = jnp.concatenate([-sin, sin], axis=0).T
        for h in range(cols // HEAD_DIM):
            lanes = slice(h * HEAD_DIM, (h + 1) * HEAD_DIM)
            q = q_in[:, lanes] + jnp.dot(scaled, wq_ref[:, lanes], preferred_element_type=F32)
            q = q * inverse + qb_ref[:, lanes]
            q_ref[:, lanes] = (q * cos + pltpu.roll(q, HALF, 1) * sin).astype(BF)

    ins = [vmem(p) for p in pieces] + [hbm(gain), hbm(wq), hbm(wkv)]
    ins += [hbm(t) for t in total] + [qb, kvb, hbm(cosine), hbm(sine)]
    in_specs = [parked(p.shape) for p in pieces] + [
        pl.BlockSpec((1, width), lambda j, s: (0, s[source])),
        pl.BlockSpec((width, cols), lambda j, s: (s[source], 0)),
        pl.BlockSpec((fresh_cols, width), lambda j, s: (0, s[source])),
    ]
    in_specs += [
        pl.BlockSpec((None,) + t.shape[1:], lambda j, s: (0, 0, 0)) for t in total
    ]
    in_specs += [whole(qb.shape), whole(kvb.shape)]
    in_specs += [
        pl.BlockSpec((None,) + t.shape[1:], lambda j, s: (block, 0, 0)) for t in (cosine, sine)
    ]
    in_specs += waits_on(waits)
    return pl.pallas_call(
        kernel,
        grid_spec=pltpu.PrefetchScalarGridSpec(
            num_scalar_prefetch=1,
            grid=(1,),
            in_specs=in_specs,
            out_specs=[whole((rows, cols)), whole((2, half, rows)), whole((2, half, rows))],
            scratch_shapes=[pltpu.VMEM((rows, width), BF)],
        ),
        out_shape=[
            pltpu.VMEM((rows, cols), BF),
            pltpu.VMEM((2, half, rows), F32),
            pltpu.VMEM((2, half, rows), BF),
        ],
        compiler_params=params(),
        cost_estimate=product_cost(rows, width, cols + fresh_cols, 1),
        name="finish_products",
    )(spots, *ins, *waits)


def cut_out(parts, waits=()):
    def kernel(*refs):
        for i in range(len(parts)):
            refs[len(parts) + len(waits) + i][...] = refs[i][...]

    shapes = [
        a.shape if lead is None else a.shape[1:-2] + (size, a.shape[-1])
        for a, lead, _, size in parts
    ]
    in_specs = [
        whole(shape)
        if lead is None
        else pl.BlockSpec(
            (None,) + shape,
            functools.partial(lambda at, _: at, (lead,) + (0,) * (a.ndim - 3) + (nth, 0)),
        )
        for (a, lead, nth, _), shape in zip(parts, shapes)
    ]
    return pl.pallas_call(
        kernel,
        grid=(1,),
        in_specs=in_specs + waits_on(waits),
        out_specs=[whole(shape) for shape in shapes],
        out_shape=[pltpu.VMEM(shape, BF) for shape in shapes],
        compiler_params=params(),
        cost_estimate=pl.CostEstimate(
            flops=0, bytes_accessed=sum(4 * math.prod(s) for s in shapes), transcendentals=0
        ),
        name="cut_out",
    )(*[a for a, *_ in parts], *waits)


class Trade:
    def __init__(self, scalars, ins, outs, run):
        self.scalars, self.ins, self.outs, self.run = scalars, ins, outs, run


def slots_for(trade_step, sections):
    bit = 1 << trade_step
    return [
        (s, s // bit % 2, s // (2 * bit) * bit + s % bit) for s in range(sections)
    ]


def pick_sent(high, slots, out, step, sections):
    for mine in range(2):

        @pl.when(high == mine)
        def _(mine=mine):
            for s, side, place in slots_for(step, sections):
                if side != mine:
                    out[place] = slots[s]


def merge_got(high, slots, got, out, step, sections):
    for mine in range(2):

        @pl.when(high == mine)
        def _(mine=mine):
            for s, side, place in slots_for(step, sections):
                out[s] = slots[s] if side == mine else got[place]


def add_up(groups, waits=(), trade=None):
    flat = [member for group in groups for member in group]
    extra_ins = [] if trade is None else trade.ins
    extra_outs = [] if trade is None else trade.outs
    scalars = jnp.zeros((1,), jnp.int32) if trade is None else trade.scalars

    def rows_of(array):
        return array.shape[-2]

    def kernel(scalar_ref, *refs):
        extra_refs = refs[len(flat) : len(flat) + len(extra_ins)]
        out_refs = refs[len(flat) + len(extra_ins) + len(waits) :]
        at = 0
        for group, out in zip(groups, out_refs):
            members = refs[at : at + len(group)]
            at += len(group)
            rows = rows_of(group[0][0])
            marks = sorted(
                {0, rows} | {f for _, f, _ in group} | {f + rows_of(a) for a, f, _ in group}
            )
            for low, high in zip(marks, marks[1:]):
                total = None
                for ref, (array, first, _) in zip(members, group):
                    if first <= low and high <= first + rows_of(array):
                        term = ref[low - first : high - first].astype(F32)
                        total = term if total is None else total + term
                out[low:high] = total.astype(BF)
        if trade is not None:
            trade.run(scalar_ref, extra_refs, out_refs[len(groups) :])

    def spec(array, kind):
        if kind is LINK:
            return IN_VMEM
        if array.ndim == 3:
            return pl.BlockSpec((None,) + array.shape[1:], lambda *_: (kind, 0, 0))
        return whole(array.shape)

    shapes = [group[0][0].shape[-2:] for group in groups] + extra_outs
    return pl.pallas_call(
        kernel,
        grid=(1,),
        in_specs=[SMEM]
        + [spec(a, kind) for a, _, kind in flat]
        + [IN_VMEM] * len(extra_ins)
        + waits_on(waits),
        out_specs=[IN_VMEM] * len(shapes),
        out_shape=[pltpu.VMEM(shape, BF) for shape in shapes],
        compiler_params=params(),
        cost_estimate=pl.CostEstimate(
            flops=sum(a.size for a, *_ in flat),
            bytes_accessed=2 * sum(a.size for a, *_ in flat),
            transcendentals=0,
        ),
        name="add_up",
    )(
        scalars,
        *[vmem(a) if kind is LINK else hbm(a) for a, _, kind in flat],
        *[vmem(a) for a in extra_ins],
        *waits,
    )


def attention(spots, block, q, kv, other, cache, cache_other, cosine, sine, waits=()):
    rows, cols = q.shape
    half = kv.shape[1]
    resident = cache.shape[3]
    heads = cols // HEAD_DIM
    factor = math.log2(math.e) / math.sqrt(HEAD_DIM)

    def kernel(flag_ref, q_ref, kv_ref, other_ref, cache_ref, mate_ref, cos_ref, sin_ref, *rest):
        out_ref, page_ref, kt, vt, kf, vf = rest[len(waits) :]
        low = flag_ref[LOWER] == 1
        cos, sin = cos_ref[...], sin_ref[...]
        mine, theirs = kv_ref[0], other_ref[0].astype(F32)
        first, second = jnp.where(low, mine, theirs), jnp.where(low, theirs, mine)
        key_first = (first * cos - second * sin).astype(BF)
        key_second = (second * cos + first * sin).astype(BF)
        kf[:half], kf[half:] = key_first, key_second
        value, value_other = kv_ref[1].astype(BF), other_ref[1]
        pages = rows // PAGE
        for p in range(pages):
            page_ref[p, 1] = value[:, p * PAGE : (p + 1) * PAGE]

        @pl.when(low)
        def _():
            for p in range(pages):
                page_ref[p, 0] = key_first[:, p * PAGE : (p + 1) * PAGE]
            vf[:half], vf[half:] = value, value_other
            kt[:half], kt[half:] = cache_ref[0], mate_ref[0]
            vt[:half], vt[half:] = cache_ref[1], mate_ref[1]

        @pl.when(jnp.logical_not(low))
        def _():
            for p in range(pages):
                page_ref[p, 0] = key_second[:, p * PAGE : (p + 1) * PAGE]
            vf[:half], vf[half:] = value_other, value
            kt[:half], kt[half:] = mate_ref[0], cache_ref[0]
            vt[:half], vt[half:] = mate_ref[1], cache_ref[1]

        seen = lax.broadcasted_iota(jnp.int32, (1, resident), 1) < flag_ref[LENGTH + block]
        shut = jnp.where(seen, 0.0, -1e30).astype(F32)
        causal = lax.broadcasted_iota(jnp.int32, (TILE, TILE), 1) <= lax.broadcasted_iota(
            jnp.int32, (TILE, TILE), 0
        )
        nt = (((1,), (1,)), ((), ()))
        for r in range(rows // TILE):
            span = slice(r * TILE, (r + 1) * TILE)
            for h in range(heads):
                lanes = slice(h * HEAD_DIM, (h + 1) * HEAD_DIM)
                qh = q_ref[span, lanes]
                s_old = jnp.dot(qh, kt[...], preferred_element_type=F32) * factor + shut
                s_new = jnp.dot(qh, kf[:, : (r + 1) * TILE], preferred_element_type=F32) * factor
                s_diag = jnp.where(causal, s_new[:, r * TILE :], -1e30)
                peak = jnp.maximum(
                    jnp.max(s_old, axis=-1, keepdims=True), jnp.max(s_diag, axis=-1, keepdims=True)
                )
                if r:
                    s_past = s_new[:, : r * TILE]
                    peak = jnp.maximum(peak, jnp.max(s_past, axis=-1, keepdims=True))
                    p_past = jnp.exp2(s_past - peak)
                p_old, p_diag = jnp.exp2(s_old - peak), jnp.exp2(s_diag - peak)
                weight = jnp.sum(p_old, axis=-1, keepdims=True) + jnp.sum(
                    p_diag, axis=-1, keepdims=True
                )
                o = lax.dot_general(p_old.astype(BF), vt[...], nt, preferred_element_type=F32)
                o += lax.dot_general(
                    p_diag.astype(BF), vf[:, span], nt, preferred_element_type=F32
                )
                if r:
                    weight += jnp.sum(p_past, axis=-1, keepdims=True)
                    o += lax.dot_general(
                        p_past.astype(BF), vf[:, : r * TILE], nt, preferred_element_type=F32
                    )
                out_ref[span, lanes] = (o / weight).astype(BF)

    ins = [vmem(q), vmem(kv), vmem(other), hbm(cache), vmem(cache_other), hbm(cosine), hbm(sine)]
    per_block = lambda t: pl.BlockSpec((None,) + t.shape[1:], lambda *_: (block,) + (0,) * (t.ndim - 1))
    pairs = heads * rows * (resident + rows // 2 + TILE // 2)
    return pl.pallas_call(
        kernel,
        grid_spec=pltpu.PrefetchScalarGridSpec(
            num_scalar_prefetch=1,
            grid=(1,),
            in_specs=[whole(a.shape) for a in ins[:3]]
            + [per_block(a) for a in ins[3:]]
            + waits_on(waits),
            out_specs=[whole((rows, cols)), whole((rows // PAGE, 2, half, PAGE))],
            scratch_shapes=[
                pltpu.VMEM((HEAD_DIM, resident), BF),
                pltpu.VMEM((HEAD_DIM, resident), BF),
                pltpu.VMEM((HEAD_DIM, rows), BF),
                pltpu.VMEM((HEAD_DIM, rows), BF),
            ],
        ),
        out_shape=[
            pltpu.VMEM((rows, cols), BF),
            pltpu.HBM((rows // PAGE, 2, half, PAGE), BF),
        ],
        compiler_params=params(),
        cost_estimate=pl.CostEstimate(
            flops=8 * pairs * HEAD_DIM, bytes_accessed=4 * rows * cols, transcendentals=2 * pairs
        ),
        name="attention",
    )(spots, *ins, *waits)


def project(spots, attended, wo, targets, cuts, waits=(), send=False):
    rows, depth = attended.shape
    width = wo.shape[1] // (2 * NZ)
    count = len(targets)
    outs = [(size, width) for cut in cuts for size in cut]

    def kernel(spot_ref, w_ref, a_ref, *refs):
        out_refs, rest = refs[len(waits) : len(waits) + len(outs)], refs[len(waits) + len(outs) :]
        w_buf, sems = rest[:2]
        copies = []
        for j in range(count):
            span = pl.ds(pl.multiple_of(spot_ref[targets[j]] * width, width), width)
            copies.append(pltpu.make_async_copy(w_ref.at[:, span], w_buf.at[j], sems.at[j]))
            copies[j].start()
        nth, leaving = 0, []
        for j in range(count):
            copies[j].wait()
            start = 0
            for size in cuts[j]:
                share = jnp.dot(
                    a_ref[start : start + size], w_buf[j], preferred_element_type=F32
                ).astype(BF)
                if send:
                    out_refs[nth][...] = share
                else:
                    rest[2][nth] = share
                    leaving.append(
                        pltpu.make_async_copy(rest[2].at[nth], out_refs[nth], rest[3].at[nth])
                    )
                    leaving[nth].start()
                start += size
                nth += 1
        for copy in leaving:
            copy.wait()

    scratch = [pltpu.VMEM((count, depth, width), BF), pltpu.SemaphoreType.DMA((count,))]
    if not send:
        scratch += [pltpu.VMEM((count, rows, width), BF), pltpu.SemaphoreType.DMA((count,))]
    return pl.pallas_call(
        kernel,
        in_specs=[SMEM, ANY, IN_VMEM] + waits_on(waits),
        out_specs=[IN_VMEM if send else ANY] * len(outs),
        out_shape=[(pltpu.VMEM if send else pltpu.HBM)(o, BF) for o in outs],
        scratch_shapes=scratch,
        compiler_params=pltpu.CompilerParams(vmem_limit_bytes=16 * 1024 * 1024),
        cost_estimate=product_cost(rows, depth, width, count),
        name="project",
    )(spots, hbm(wo), vmem(attended), *waits)


def tables(places, row_count):
    position = places.astype(F32)[:, None] + jnp.arange(row_count, dtype=F32)
    frequency = jnp.exp(jnp.arange(HALF, dtype=F32) * (-2.0 * math.log(1000000.0) / HEAD_DIM))
    angles = frequency[None, :, None] * position[:, None, :]
    return jnp.cos(angles), jnp.sin(angles)


def put_block(into, block, place, blocks):
    old = [] if into is None else [hbm(into)]

    def kernel(place_ref, block_ref, *refs):
        refs[-1][...] = block_ref[...]

    return pl.pallas_call(
        kernel,
        grid_spec=pltpu.PrefetchScalarGridSpec(
            num_scalar_prefetch=1,
            grid=(1,),
            in_specs=[IN_VMEM] + waits_on(old),
            out_specs=[pl.BlockSpec((None,) + block.shape, lambda _, p: (p[0], 0, 0))],
        ),
        out_shape=[pltpu.HBM((blocks,) + block.shape, BF)],
        input_output_aliases={2: 0} if old else {},
        compiler_params=params(),
        cost_estimate=pl.CostEstimate(
            flops=0, bytes_accessed=4 * block.size, transcendentals=0
        ),
        name="put_block",
    )(place[None], vmem(block), *old)


def trade_alone(trade, waits, keep, cost):
    def kernel(scalar_ref, *refs):
        trade.run(scalar_ref, refs[: len(trade.ins)], refs[len(trade.ins) + len(waits) :])

    return pl.pallas_call(
        kernel,
        in_specs=[SMEM] + [IN_VMEM] * len(trade.ins) + waits_on(waits),
        out_specs=[IN_VMEM] * len(trade.outs),
        out_shape=[keep(shape, BF) for shape in trade.outs],
        compiler_params=pltpu.CompilerParams(vmem_limit_bytes=16 * 1024 * 1024),
        cost_estimate=cost,
        name="trade_pages",
    )(trade.scalars, *[vmem(a) for a in trade.ins], *waits)


def local(
    hidden,
    norm_gain,
    query_weight,
    query_bias,
    key_value_weight,
    key_value_bias,
    output_weight,
    resident_cache,
    resident_length,
    plan,
    page_owner,
):
    rows_all = hidden[0]
    blocks, rows, width = rows_all.shape
    wq, wo = query_weight[0], output_weight[0]
    half = key_value_weight.shape[3]
    wkv = jnp.swapaxes(key_value_weight[0], 1, 2).reshape(2 * half, -1)
    me = lax.axis_index("tensor")
    y, z = me // NZ, me % NZ
    lower = z % 2 == 0
    sections = lax.axis_size("segment")
    onward = [(i, (i + 1) % sections) for i in range(sections)]

    def at(flip, shift):
        return flip * NZ + shift % NZ

    spots = jnp.concatenate(
        [
            jnp.stack([(y + f) % 2 * NZ + (z + d) % NZ for f in range(2) for d in range(NZ)]),
            lower.astype(jnp.int32)[None],
            resident_length[0],
        ]
    ).astype(jnp.int32)

    gain = norm_gain.astype(F32)
    qb = query_bias.astype(F32)
    kvb = key_value_bias.astype(F32).reshape(1, 2 * half)
    cosine, sine = tables(resident_length[0], rows)
    caches = jnp.swapaxes(resident_cache[0], 2, 3)

    plan_before = lax.ppermute(plan[0], "segment", onward)
    place = (plan_before[0] != 0).astype(jnp.int32)

    from_below, from_across, from_above = up(rows_all), across(rows_all), down(rows_all)
    far, diag_down, diag_up = up(from_below), across(from_below), down(from_across)
    total = add_products(
        spots,
        [hbm(rows_all), from_below, from_across, from_above],
        [at(0, 0), at(0, -1), at(1, 0), at(0, 1)],
        gain,
        wq,
        wkv,
        None,
        (hbm(cosine), hbm(sine), hbm(plan_before)),
    )
    quarter, cut = rows // 4, rows // 2
    low_rows, high_rows, far_rows = cut_out(
        [(diag_down, 0, 0, quarter), (diag_up, 0, 1, quarter), (far, 0, 1, cut)], [hbm(total[0])]
    )

    def mate(a):
        return lax.ppermute(a, "tensor", MATE)

    def second(b, waits):
        return add_products(
            spots,
            [far, diag_down, diag_up],
            [at(0, 2), at(1, -1), at(1, 1)],
            gain,
            wq,
            wkv,
            total,
            waits,
            b,
        )

    total0 = second(0, [vmem(low_rows)])
    low_rows, high_rows, far_rows = up(low_rows), down(high_rows), across(far_rows)
    far_second, cache_other = cut_out(
        [(far, 1, 0, rows), (hbm(caches), None, 0, 0)],
        [vmem(low_rows), vmem(high_rows), hbm(total0[0])],
    )
    cache_sent = cache_other
    cache_other, far_second = mate(cache_other), across(far_second)

    def ready(b, last, total, waits):
        q, kv, send = finish_products(
            spots, b, last, at(1, 2), gain, wq, wkv, total, qb, kvb, cosine, sine, waits
        )
        return q, kv, mate(send)

    def attend(b, q, kv, other, waits):
        return attention(
            spots, b, q, kv, other, caches, cache_other, cosine, sine, waits
        )

    def begin(attended):
        return project(spots, attended, wo, [at(1, 2)], [[cut, rows - cut]], send=True)

    def next_three(attended, waits):
        targets = [at(0, 2), at(1, 1), at(1, -1)]
        return project(spots, attended, wo, targets, [[rows]] * 3, waits)

    def last_four(attended, waits):
        targets = [at(0, -1), at(0, 1), at(1, 0), at(0, 0)]
        return project(spots, attended, wo, targets, [[rows]] * 4, waits)

    def fan(a, b, c):
        return down(a), up(b), across(c)

    q0, kv0, other0 = ready(0, [low_rows, high_rows, far_rows], total0, [vmem(cache_sent)])
    total1 = second(1, [vmem(kv0)])
    attended0, pages0 = attend(0, q0, kv0, other0, [hbm(total1[0])])
    low, high = begin(attended0)
    q1, kv1, other1 = ready(1, [far_second], total1, [vmem(low)])
    low, high = down(low), up(high)
    a_, b_, c_ = next_three(attended0, [vmem(kv1)])
    a_, b_, c_ = add_up(
        [
            [(a_, 0, HERE)],
            [(b_, 0, HERE), (high, cut, LINK)],
            [(c_, 0, HERE), (low, 0, LINK)],
        ],
        [vmem(other1)],
    )
    d_, e_, g_, own0 = last_four(attended0, [vmem(c_)])
    a_, b_, c_ = fan(a_, b_, c_)
    attended1, pages1 = attend(1, q1, kv1, other1, [hbm(own0)])
    me_there = lax.axis_index("segment").astype(jnp.int32)
    page = pages0.shape[1:]
    all_slots, half_slots = (sections,) + page, (sections // 2,) + page
    pages_each = pages0.shape[0]
    bits = [me_there // 2**k % 2 for k in range(4)]

    def first_trade(scalar_ref, ins, outs):
        slots, sent = outs
        for o in range(sections):
            slots[o] = jnp.zeros(page, BF)
        for p in range(blocks * pages_each):
            slots[scalar_ref[1 + p]] = ins[p // pages_each][p % pages_each]
        pick_sent(scalar_ref[0], slots, sent, 0, sections)

    def later_trade(before, step):
        def run(scalar_ref, ins, outs):
            merge_got(scalar_ref[0], ins[0], ins[1], outs[0], before, sections)
            pick_sent(scalar_ref[1], outs[0], outs[1], step, sections)

        return run

    def last_trade(scalar_ref, ins, outs):
        merge_got(scalar_ref[0], ins[0], ins[1], outs[0], 1, sections)

    def trade_with(sent, step):
        return lax.ppermute(sent, "segment", [(i, i ^ 1 << step) for i in range(sections)])

    low1, high1 = begin(attended1)
    a1, b1, c1 = next_three(attended1, [vmem(low1)])
    low1, high1 = down(low1), up(high1)
    trade = Trade(
        jnp.concatenate([bits[0][None], page_owner[0]]),
        [pages0, pages1],
        [all_slots, half_slots],
        first_trade,
    )
    d_, e_, g_, slots, sent = add_up(
        [
            [(d_, 0, HERE), (a_, 0, LINK), (c_, 0, LINK)],
            [(e_, 0, HERE)],
            [(g_, 0, HERE), (b_, 0, LINK)],
        ],
        [hbm(c1)],
        trade,
    )
    d_, e_, g_ = fan(d_, e_, g_)
    got = trade_with(sent, 0)
    trade = Trade(
        jnp.stack([bits[0], bits[2]]), [slots, got], [all_slots, half_slots], later_trade(0, 2)
    )
    a1, b1, c1, done0, slots, sent = add_up(
        [
            [(a1, 0, HERE)],
            [(b1, 0, HERE), (high1, cut, LINK)],
            [(c1, 0, HERE), (low1, 0, LINK)],
            [(rows_all, 0, 0), (own0, 0, HERE), (e_, 0, LINK), (d_, 0, LINK), (g_, 0, LINK)],
        ],
        (),
        trade,
    )
    a1, b1, c1 = fan(a1, b1, c1)
    first = lax.ppermute(done0, "segment", onward)
    got = trade_with(sent, 2)
    d1, e1, g1, own1 = last_four(attended1, [vmem(got)])
    (next_hidden,) = put_block(None, first, place, blocks)
    trade = Trade(
        jnp.stack([bits[2], bits[3]]), [slots, got], [all_slots, half_slots], later_trade(2, 3)
    )
    d1, e1, g1, slots, sent = add_up(
        [
            [(d1, 0, HERE), (a1, 0, LINK), (c1, 0, LINK)],
            [(e1, 0, HERE)],
            [(g1, 0, HERE), (b1, 0, LINK)],
        ],
        [hbm(next_hidden)],
        trade,
    )
    d1, e1, g1 = fan(d1, e1, g1)
    got = trade_with(sent, 3)
    trade = Trade(
        jnp.stack([bits[3], bits[1]]), [slots, got], [all_slots, half_slots], later_trade(3, 1)
    )
    done1, slots, sent = add_up(
        [[(rows_all, 0, 1), (own1, 0, HERE), (e1, 0, LINK), (d1, 0, LINK), (g1, 0, LINK)]],
        (),
        trade,
    )
    got = trade_with(sent, 1)
    last = lax.ppermute(done1, "segment", onward)
    (shipped,) = trade_alone(
        Trade(bits[1][None], [slots, got], [all_slots], last_trade), (), pltpu.HBM, HEAVY
    )
    (next_hidden,) = put_block(next_hidden, last, 1 - place, blocks)
    return next_hidden[None], jnp.swapaxes(shipped, 2, 3)[None]


def solution(mesh):
    return jax.shard_map(
        local,
        mesh=mesh,
        in_specs=(
            P("segment", None, None, "tensor"),
            P("segment", None),
            P("segment", None, "tensor"),
            P("segment", "tensor"),
            P("segment", None, None, "tensor"),
            P("segment", None, "tensor"),
            P("segment", "tensor", None),
            P("segment", None, None, None, "tensor"),
            P("segment", None),
            P("segment", None),
            P("segment", None),
        ),
        out_specs=(P("segment", None, None, "tensor"), P("segment", None, None, None, "tensor")),
        check_vma=False,
    )
```

```python
import functools
import math

import jax
import jax.numpy as jnp
from jax import lax
from jax.experimental import pallas as pl
from jax.experimental.pallas import tpu as pltpu
from jax.sharding import PartitionSpec as P

HEAD_DIM = 128
LINK, LOOSE, HERE = "link", "loose", 0
LOWER, LENGTH = 8, 9
HALF = HEAD_DIM // 2
PAGE = 128
EPSILON = 1e-06
NZ = 4
TILE = 128
BF = jnp.bfloat16
F32 = jnp.float32

UP = [(y * NZ + z, y * NZ + (z + 1) % NZ) for y in range(2) for z in range(NZ)]
DOWN = [(y * NZ + z, y * NZ + (z - 1) % NZ) for y in range(2) for z in range(NZ)]
ACROSS = [(y * NZ + z, (1 - y) * NZ + z) for y in range(2) for z in range(NZ)]
MATE = [(i, i ^ 1) for i in range(2 * NZ)]

ANY = pl.BlockSpec(memory_space=pl.ANY)


def up(a):
    return lax.ppermute(a, "tensor", UP)


def down(a):
    return lax.ppermute(a, "tensor", DOWN)


def across(a):
    return lax.ppermute(a, "tensor", ACROSS)


def whole(shape):
    return pl.BlockSpec(shape, lambda *_: (0,) * len(shape))


def params(grid_dims=1, mebibytes=16):
    return pltpu.CompilerParams(
        vmem_limit_bytes=mebibytes * 1024 * 1024, dimension_semantics=("arbitrary",) * grid_dims
    )


def hbm(a):
    return pltpu.with_memory_space_constraint(a, pltpu.HBM)


def vmem(a):
    return pltpu.with_memory_space_constraint(a, pltpu.VMEM)


IN_VMEM = pl.BlockSpec(memory_space=pltpu.VMEM)
SMEM = pl.BlockSpec(memory_space=pltpu.SMEM)


def waits_on(waits):
    return [ANY] * len(waits)


def parked(shape, index=None):
    index = (0,) * len(shape) if index is None else index
    return pl.BlockSpec(shape, lambda *_: index, pipeline_mode=pl.Buffered(1))


def product_cost(rows, width, columns, count):
    return pl.CostEstimate(
        flops=2 * rows * width * columns * count,
        bytes_accessed=2 * width * (rows + columns) * count + 8 * rows * columns,
        transcendentals=0,
    )


NT = (((1,), (1,)), ((), ()))


def fold(squared):
    total = squared[:, :HEAD_DIM]
    for start in range(HEAD_DIM, squared.shape[1], HEAD_DIM):
        total = total + squared[:, start : start + HEAD_DIM]
    return total


def add_products(spots, shards, sources, gain, wq, wkv, total, waits=(), only=None):
    count = len(shards)
    blocks, rows, width = shards[0].shape
    place = (0, 0, 0)
    if only is not None:
        blocks, place = 1, (only, 0, 0)
    cols = wq.shape[1]
    fresh_cols = wkv.shape[0]
    first = total is None

    def pick(spot_ref, step):
        chosen = spot_ref[sources[0]]
        for j in range(1, count):
            chosen = jnp.where(step == j, spot_ref[sources[j]], chosen)
        return chosen

    ins = list(shards) + [hbm(gain), hbm(wq), hbm(wkv)]
    ins += ([] if first else [hbm(t) for t in total]) + list(waits)

    def kernel(src_ref, *refs):
        g_ref, wq_ref, wkv_ref = refs[count : count + 3]
        before, after = refs[count + 3 : count + 6], refs[-3:]
        for j in range(count):

            @pl.when(pl.program_id(0) == j)
            def _(j=j):
                x = refs[j][...].reshape(blocks * rows, width).astype(F32)
                scaled = (x * g_ref[...]).astype(BF)
                more = (
                    jnp.dot(scaled, wq_ref[...], preferred_element_type=F32),
                    lax.dot_general(scaled, wkv_ref[...], NT, preferred_element_type=F32),
                    fold(x * x),
                )
                for old, new, term in zip(after if j else before, after, more):
                    term = term.reshape(new.shape)
                    new[...] = term if j == 0 and first else old[...] + term

    shapes = [(blocks, rows, cols), (blocks, rows, fresh_cols), (blocks, rows, HEAD_DIM)]
    in_specs = [parked((blocks, rows, width), place)] * count + [
        pl.BlockSpec((1, width), lambda j, s: (0, pick(s, j))),
        pl.BlockSpec((width, cols), lambda j, s: (pick(s, j), 0)),
        pl.BlockSpec((fresh_cols, width), lambda j, s: (0, pick(s, j))),
    ]
    in_specs += [] if first else [parked(shape, place) for shape in shapes]
    in_specs += waits_on(waits)
    return pl.pallas_call(
        kernel,
        grid_spec=pltpu.PrefetchScalarGridSpec(
            num_scalar_prefetch=1,
            grid=(count,),
            in_specs=in_specs,
            out_specs=[parked(shape) for shape in shapes],
        ),
        out_shape=[pltpu.HBM(shape, F32) for shape in shapes],
        compiler_params=params(1, 32),
        cost_estimate=product_cost(blocks * rows, width, cols + fresh_cols, count),
        name="add_products",
    )(spots, *ins)


def finish_products(spots, block, pieces, source, gain, wq, wkv, total, qb, kvb, cosine, sine, waits=()):
    width = pieces[0].shape[1]
    sizes = [p.shape[0] for p in pieces]
    rows = sum(sizes)
    cols = wq.shape[1]
    fresh_cols = wkv.shape[0]
    half = fresh_cols // 2
    count = len(pieces)
    model = wq.shape[0]

    def kernel(src_ref, *refs):
        g_ref, wq_ref, wkv_ref, q_in, kv_in, sq_in, qb_ref, kvb_ref, cos_ref, sin_ref = refs[
            count : count + 10
        ]
        q_ref, kv_ref, send_ref, x_ref = refs[-4:]
        start = 0
        for piece, size in zip(refs[:count], sizes):
            x_ref[start : start + size] = piece[...]
            start += size
        x = x_ref[...].astype(F32)
        squares = jnp.sum(sq_in[...] + fold(x * x), axis=-1, keepdims=True)
        inverse = lax.rsqrt(squares / model + EPSILON)
        x_ref[...] = (x * g_ref[...]).astype(BF)
        scaled = x_ref[...]
        kv = kv_in[...] + lax.dot_general(scaled, wkv_ref[...], NT, preferred_element_type=F32)
        kv = (kv * inverse + kvb_ref[...]).T.reshape(2, half, rows)
        kv_ref[...] = kv
        send_ref[...] = kv.astype(BF)
        cos, sin = cos_ref[...], sin_ref[...]
        cos = jnp.concatenate([cos, cos], axis=0).T
        sin = jnp.concatenate([-sin, sin], axis=0).T
        for h in range(cols // HEAD_DIM):
            lanes = slice(h * HEAD_DIM, (h + 1) * HEAD_DIM)
            q = q_in[:, lanes] + jnp.dot(scaled, wq_ref[:, lanes], preferred_element_type=F32)
            q = q * inverse + qb_ref[:, lanes]
            q_ref[:, lanes] = (q * cos + pltpu.roll(q, HALF, 1) * sin).astype(BF)

    ins = [vmem(p) for p in pieces] + [hbm(gain), hbm(wq), hbm(wkv)]
    ins += [hbm(t) for t in total] + [qb, kvb, hbm(cosine), hbm(sine)]
    in_specs = [parked(p.shape) for p in pieces] + [
        pl.BlockSpec((1, width), lambda j, s: (0, s[source])),
        pl.BlockSpec((width, cols), lambda j, s: (s[source], 0)),
        pl.BlockSpec((fresh_cols, width), lambda j, s: (0, s[source])),
    ]
    in_specs += [
        pl.BlockSpec((None,) + t.shape[1:], lambda j, s: (0, 0, 0)) for t in total
    ]
    in_specs += [whole(qb.shape), whole(kvb.shape)]
    in_specs += [
        pl.BlockSpec((None,) + t.shape[1:], lambda j, s: (block, 0, 0)) for t in (cosine, sine)
    ]
    in_specs += waits_on(waits)
    return pl.pallas_call(
        kernel,
        grid_spec=pltpu.PrefetchScalarGridSpec(
            num_scalar_prefetch=1,
            grid=(1,),
            in_specs=in_specs,
            out_specs=[whole((rows, cols)), whole((2, half, rows)), whole((2, half, rows))],
            scratch_shapes=[pltpu.VMEM((rows, width), BF)],
        ),
        out_shape=[
            pltpu.VMEM((rows, cols), BF),
            pltpu.VMEM((2, half, rows), F32),
            pltpu.VMEM((2, half, rows), BF),
        ],
        compiler_params=params(),
        cost_estimate=product_cost(rows, width, cols + fresh_cols, 1),
        name="finish_products",
    )(spots, *ins, *waits)


def cut_out(parts, waits=()):
    def kernel(*refs):
        for i in range(len(parts)):
            refs[len(parts) + len(waits) + i][...] = refs[i][...]

    shapes = [
        a.shape if lead is None else a.shape[1:-2] + (size, a.shape[-1])
        for a, lead, _, size in parts
    ]
    in_specs = [
        whole(shape)
        if lead is None
        else pl.BlockSpec(
            (None,) + shape,
            functools.partial(lambda at, _: at, (lead,) + (0,) * (a.ndim - 3) + (nth, 0)),
        )
        for (a, lead, nth, _), shape in zip(parts, shapes)
    ]
    return pl.pallas_call(
        kernel,
        grid=(1,),
        in_specs=in_specs + waits_on(waits),
        out_specs=[whole(shape) for shape in shapes],
        out_shape=[pltpu.VMEM(shape, BF) for shape in shapes],
        compiler_params=params(),
        cost_estimate=pl.CostEstimate(
            flops=0, bytes_accessed=sum(4 * math.prod(s) for s in shapes), transcendentals=0
        ),
        name="cut_out",
    )(*[a for a, *_ in parts], *waits)


class Trade:
    def __init__(self, scalars, ins, outs, run):
        self.scalars, self.ins, self.outs, self.run = scalars, ins, outs, run


def slots_for(trade_step, sections):
    bit = 1 << trade_step
    return [
        (s, s // bit % 2, s // (2 * bit) * bit + s % bit) for s in range(sections)
    ]


def pick_sent(high, slots, out, step, sections):
    for mine in range(2):

        @pl.when(high == mine)
        def _(mine=mine):
            for s, side, place in slots_for(step, sections):
                if side != mine:
                    out[place] = slots[s]


def merge_got(high, slots, got, out, step, sections):
    for mine in range(2):

        @pl.when(high == mine)
        def _(mine=mine):
            for s, side, place in slots_for(step, sections):
                out[s] = slots[s] if side == mine else got[place]


def add_up(groups, waits=(), trade=None, halves=1):
    flat = [member for group in groups for member in group]
    extra_ins = [] if trade is None else trade.ins
    extra_outs = [] if trade is None else trade.outs
    scalars = jnp.zeros((1,), jnp.int32) if trade is None else trade.scalars

    def rows_of(array):
        return array.shape[-2]

    def kernel(scalar_ref, *refs):
        extra_refs = refs[len(flat) : len(flat) + len(extra_ins)]
        out_refs = refs[len(flat) + len(extra_ins) + len(waits) :]
        at = 0
        for nth, group in enumerate(groups):
            members = refs[at : at + len(group)]
            at += len(group)
            rows = rows_of(group[0][0])
            part = rows // halves
            marks = sorted(
                {0, part, rows} | {f for _, f, _ in group} | {f + rows_of(a) for a, f, _ in group}
            )
            for low, high in zip(marks, marks[1:]):
                total = None
                for ref, (array, first, _) in zip(members, group):
                    if first <= low and high <= first + rows_of(array):
                        term = ref[low - first : high - first].astype(F32)
                        total = term if total is None else total + term
                out = out_refs[nth * halves + low // part]
                out[low % part : low % part + high - low] = total.astype(BF)
        if trade is not None:
            trade.run(scalar_ref, extra_refs, out_refs[len(sums) :])

    def spec(array, kind):
        if kind is LINK:
            return IN_VMEM
        if array.ndim == 3:
            return pl.BlockSpec((None,) + array.shape[1:], lambda *_: (kind, 0, 0))
        return whole(array.shape)

    def placed(array, kind):
        return vmem(array) if kind is LINK else array if kind is LOOSE else hbm(array)

    sums = [
        (rows_of(group[0][0]) // halves, group[0][0].shape[-1])
        for group in groups
        for _ in range(halves)
    ]
    return pl.pallas_call(
        kernel,
        grid=(1,),
        in_specs=[SMEM]
        + [spec(a, kind) for a, _, kind in flat]
        + [whole(a.shape) for a in extra_ins]
        + waits_on(waits),
        out_specs=[IN_VMEM] * len(sums) + [whole(shape) for shape in extra_outs],
        out_shape=[pltpu.VMEM(shape, BF) for shape in sums]
        + [pltpu.HBM(shape, BF) for shape in extra_outs],
        compiler_params=params(),
        cost_estimate=pl.CostEstimate(
            flops=sum(a.size for a, *_ in flat),
            bytes_accessed=2 * sum(a.size for a, *_ in flat),
            transcendentals=0,
        ),
        name="add_up",
    )(
        scalars,
        *[placed(a, kind) for a, _, kind in flat],
        *extra_ins,
        *waits,
    )


def attention(spots, block, q, kv, other, cache, cache_other, cosine, sine, waits=()):
    rows, cols = q.shape
    half = kv.shape[1]
    resident = cache.shape[3]
    heads = cols // HEAD_DIM
    factor = math.log2(math.e) / math.sqrt(HEAD_DIM)

    def kernel(flag_ref, q_ref, kv_ref, other_ref, cache_ref, mate_ref, cos_ref, sin_ref, *rest):
        out_ref, page_ref, kt, vt, kf, vf = rest[len(waits) :]
        low = flag_ref[LOWER] == 1
        cos, sin = cos_ref[...], sin_ref[...]
        mine, theirs = kv_ref[0], other_ref[0].astype(F32)
        first, second = jnp.where(low, mine, theirs), jnp.where(low, theirs, mine)
        key_first = (first * cos - second * sin).astype(BF)
        key_second = (second * cos + first * sin).astype(BF)
        kf[:half], kf[half:] = key_first, key_second
        value, value_other = kv_ref[1].astype(BF), other_ref[1]
        pages = rows // PAGE
        for p in range(pages):
            page_ref[p, 1] = value[:, p * PAGE : (p + 1) * PAGE]

        @pl.when(low)
        def _():
            for p in range(pages):
                page_ref[p, 0] = key_first[:, p * PAGE : (p + 1) * PAGE]
            vf[:half], vf[half:] = value, value_other
            kt[:half], kt[half:] = cache_ref[0], mate_ref[0]
            vt[:half], vt[half:] = cache_ref[1], mate_ref[1]

        @pl.when(jnp.logical_not(low))
        def _():
            for p in range(pages):
                page_ref[p, 0] = key_second[:, p * PAGE : (p + 1) * PAGE]
            vf[:half], vf[half:] = value_other, value
            kt[:half], kt[half:] = mate_ref[0], cache_ref[0]
            vt[:half], vt[half:] = mate_ref[1], cache_ref[1]

        seen = lax.broadcasted_iota(jnp.int32, (1, resident), 1) < flag_ref[LENGTH + block]
        shut = jnp.where(seen, 0.0, -1e30).astype(F32)
        causal = lax.broadcasted_iota(jnp.int32, (TILE, TILE), 1) <= lax.broadcasted_iota(
            jnp.int32, (TILE, TILE), 0
        )
        nt = (((1,), (1,)), ((), ()))
        for r in range(rows // TILE):
            span = slice(r * TILE, (r + 1) * TILE)
            for h in range(heads):
                lanes = slice(h * HEAD_DIM, (h + 1) * HEAD_DIM)
                qh = q_ref[span, lanes]
                s_old = jnp.dot(qh, kt[...], preferred_element_type=F32) * factor + shut
                s_new = jnp.dot(qh, kf[:, : (r + 1) * TILE], preferred_element_type=F32) * factor
                s_diag = jnp.where(causal, s_new[:, r * TILE :], -1e30)
                peak = jnp.maximum(
                    jnp.max(s_old, axis=-1, keepdims=True), jnp.max(s_diag, axis=-1, keepdims=True)
                )
                if r:
                    s_past = s_new[:, : r * TILE]
                    peak = jnp.maximum(peak, jnp.max(s_past, axis=-1, keepdims=True))
                    p_past = jnp.exp2(s_past - peak)
                p_old, p_diag = jnp.exp2(s_old - peak), jnp.exp2(s_diag - peak)
                weight = jnp.sum(p_old, axis=-1, keepdims=True) + jnp.sum(
                    p_diag, axis=-1, keepdims=True
                )
                o = lax.dot_general(p_old.astype(BF), vt[...], nt, preferred_element_type=F32)
                o += lax.dot_general(
                    p_diag.astype(BF), vf[:, span], nt, preferred_element_type=F32
                )
                if r:
                    weight += jnp.sum(p_past, axis=-1, keepdims=True)
                    o += lax.dot_general(
                        p_past.astype(BF), vf[:, : r * TILE], nt, preferred_element_type=F32
                    )
                out_ref[span, lanes] = (o / weight).astype(BF)

    ins = [vmem(q), vmem(kv), vmem(other), hbm(cache), vmem(cache_other), hbm(cosine), hbm(sine)]
    per_block = lambda t: pl.BlockSpec((None,) + t.shape[1:], lambda *_: (block,) + (0,) * (t.ndim - 1))
    pairs = heads * rows * (resident + rows // 2 + TILE // 2)
    return pl.pallas_call(
        kernel,
        grid_spec=pltpu.PrefetchScalarGridSpec(
            num_scalar_prefetch=1,
            grid=(1,),
            in_specs=[whole(a.shape) for a in ins[:3]]
            + [per_block(a) for a in ins[3:]]
            + waits_on(waits),
            out_specs=[whole((rows, cols)), whole((rows // PAGE, 2, half, PAGE))],
            scratch_shapes=[
                pltpu.VMEM((HEAD_DIM, resident), BF),
                pltpu.VMEM((HEAD_DIM, resident), BF),
                pltpu.VMEM((HEAD_DIM, rows), BF),
                pltpu.VMEM((HEAD_DIM, rows), BF),
            ],
        ),
        out_shape=[
            pltpu.VMEM((rows, cols), BF),
            pltpu.HBM((rows // PAGE, 2, half, PAGE), BF),
        ],
        compiler_params=params(),
        cost_estimate=pl.CostEstimate(
            flops=8 * pairs * HEAD_DIM, bytes_accessed=4 * rows * cols, transcendentals=2 * pairs
        ),
        name="attention",
    )(spots, *ins, *waits)


def project(spots, attended, wo, targets, cuts, waits=(), send=False):
    rows, depth = attended.shape
    width = wo.shape[1] // (2 * NZ)
    count = len(targets)
    outs = [(size, width) for cut in cuts for size in cut]

    def kernel(spot_ref, w_ref, a_ref, *refs):
        out_refs, rest = refs[len(waits) : len(waits) + len(outs)], refs[len(waits) + len(outs) :]
        w_buf, sems = rest[:2]
        copies = []
        for j in range(count):
            span = pl.ds(pl.multiple_of(spot_ref[targets[j]] * width, width), width)
            copies.append(pltpu.make_async_copy(w_ref.at[:, span], w_buf.at[j], sems.at[j]))
            copies[j].start()
        nth, leaving = 0, []
        for j in range(count):
            copies[j].wait()
            start = 0
            for size in cuts[j]:
                share = jnp.dot(
                    a_ref[start : start + size], w_buf[j], preferred_element_type=F32
                ).astype(BF)
                if send:
                    out_refs[nth][...] = share
                else:
                    rest[2][nth] = share
                    leaving.append(
                        pltpu.make_async_copy(rest[2].at[nth], out_refs[nth], rest[3].at[nth])
                    )
                    leaving[nth].start()
                start += size
                nth += 1
        for copy in leaving:
            copy.wait()

    scratch = [pltpu.VMEM((count, depth, width), BF), pltpu.SemaphoreType.DMA((count,))]
    if not send:
        scratch += [pltpu.VMEM((count, rows, width), BF), pltpu.SemaphoreType.DMA((count,))]
    return pl.pallas_call(
        kernel,
        in_specs=[SMEM, ANY, IN_VMEM] + waits_on(waits),
        out_specs=[IN_VMEM if send else ANY] * len(outs),
        out_shape=[(pltpu.VMEM if send else pltpu.HBM)(o, BF) for o in outs],
        scratch_shapes=scratch,
        compiler_params=pltpu.CompilerParams(vmem_limit_bytes=16 * 1024 * 1024),
        cost_estimate=product_cost(rows, depth, width, count),
        name="project",
    )(spots, hbm(wo), vmem(attended), *waits)


def tables(places, row_count):
    position = places.astype(F32)[:, None] + jnp.arange(row_count, dtype=F32)
    frequency = jnp.exp(jnp.arange(HALF, dtype=F32) * (-2.0 * math.log(1000000.0) / HEAD_DIM))
    angles = frequency[None, :, None] * position[:, None, :]
    return jnp.cos(angles), jnp.sin(angles)


def put_block(into, parts, place, blocks):
    old = [] if into is None else [hbm(into)]
    size = parts[0].shape[0]
    shape = (size * len(parts), parts[0].shape[1])

    def kernel(place_ref, *refs):
        for i in range(len(parts)):
            refs[-1][i * size : (i + 1) * size] = refs[i][...]

    return pl.pallas_call(
        kernel,
        grid_spec=pltpu.PrefetchScalarGridSpec(
            num_scalar_prefetch=1,
            grid=(1,),
            in_specs=[IN_VMEM] * len(parts) + waits_on(old),
            out_specs=[pl.BlockSpec((None,) + shape, lambda _, p: (p[0], 0, 0))],
        ),
        out_shape=[pltpu.HBM((blocks,) + shape, BF)],
        input_output_aliases={1 + len(parts): 0} if old else {},
        compiler_params=params(),
        cost_estimate=pl.CostEstimate(
            flops=0, bytes_accessed=4 * math.prod(shape), transcendentals=0
        ),
        name="put_block",
    )(place[None], *[vmem(p) for p in parts], *old)


def trade_alone(trade, waits):
    def kernel(scalar_ref, *refs):
        trade.run(scalar_ref, refs[: len(trade.ins)], refs[len(trade.ins) + len(waits) :])

    return pl.pallas_call(
        kernel,
        in_specs=[SMEM] + [IN_VMEM] * len(trade.ins) + waits_on(waits),
        out_specs=[IN_VMEM] * len(trade.outs),
        out_shape=[pltpu.HBM(shape, BF) for shape in trade.outs],
        compiler_params=pltpu.CompilerParams(vmem_limit_bytes=16 * 1024 * 1024),
        cost_estimate=pl.CostEstimate(flops=0, bytes_accessed=2**20, transcendentals=0),
        name="trade_pages",
    )(trade.scalars, *trade.ins, *waits)


def local(
    hidden,
    norm_gain,
    query_weight,
    query_bias,
    key_value_weight,
    key_value_bias,
    output_weight,
    resident_cache,
    resident_length,
    plan,
    page_owner,
):
    rows_all = hidden[0]
    blocks, rows, width = rows_all.shape
    wq, wo = query_weight[0], output_weight[0]
    half = key_value_weight.shape[3]
    wkv = jnp.swapaxes(key_value_weight[0], 1, 2).reshape(2 * half, -1)
    me = lax.axis_index("tensor")
    y, z = me // NZ, me % NZ
    lower = z % 2 == 0
    sections = lax.axis_size("segment")
    onward = [(i, (i + 1) % sections) for i in range(sections)]

    def at(flip, shift):
        return flip * NZ + shift % NZ

    spots = jnp.concatenate(
        [
            jnp.stack([(y + f) % 2 * NZ + (z + d) % NZ for f in range(2) for d in range(NZ)]),
            lower.astype(jnp.int32)[None],
            resident_length[0],
        ]
    ).astype(jnp.int32)

    gain = norm_gain.astype(F32)
    qb = query_bias.astype(F32)
    kvb = key_value_bias.astype(F32).reshape(1, 2 * half)
    cosine, sine = tables(resident_length[0], rows)
    caches = jnp.swapaxes(resident_cache[0], 2, 3)

    plan_before = lax.ppermute(plan[0], "segment", onward)
    place = (plan_before[0] != 0).astype(jnp.int32)

    from_below, from_across, from_above = up(rows_all), across(rows_all), down(rows_all)
    far, diag_down, diag_up = up(from_below), across(from_below), down(from_across)
    total = add_products(
        spots,
        [hbm(rows_all), from_below, from_across, from_above],
        [at(0, 0), at(0, -1), at(1, 0), at(0, 1)],
        gain,
        wq,
        wkv,
        None,
        (hbm(cosine), hbm(sine), hbm(plan_before)),
    )
    quarter, cut = rows // 4, rows // 2
    low_rows, high_rows, far_rows = cut_out(
        [(diag_down, 0, 0, quarter), (diag_up, 0, 1, quarter), (far, 0, 1, cut)], [hbm(total[0])]
    )

    def mate(a):
        return lax.ppermute(a, "tensor", MATE)

    def second(b, waits):
        return add_products(
            spots,
            [far, diag_down, diag_up],
            [at(0, 2), at(1, -1), at(1, 1)],
            gain,
            wq,
            wkv,
            total,
            waits,
            b,
        )

    total0 = second(0, [vmem(low_rows)])
    low_rows, high_rows, far_rows = up(low_rows), down(high_rows), across(far_rows)
    far_second, cache_other = cut_out(
        [(far, 1, 0, rows), (hbm(caches), None, 0, 0)],
        [vmem(low_rows), vmem(high_rows), hbm(total0[0])],
    )
    cache_sent = cache_other
    cache_other, far_second = mate(cache_other), across(far_second)

    def ready(b, last, total, waits):
        q, kv, send = finish_products(
            spots, b, last, at(1, 2), gain, wq, wkv, total, qb, kvb, cosine, sine, waits
        )
        return q, kv, mate(send)

    def attend(b, q, kv, other, waits):
        return attention(
            spots, b, q, kv, other, caches, cache_other, cosine, sine, waits
        )

    def begin(attended):
        return project(spots, attended, wo, [at(1, 2)], [[cut, rows - cut]], send=True)

    def next_three(attended, waits):
        targets = [at(0, 2), at(1, 1), at(1, -1)]
        return project(spots, attended, wo, targets, [[rows]] * 3, waits)

    def last_four(attended, waits):
        targets = [at(0, -1), at(0, 1), at(1, 0), at(0, 0)]
        return project(spots, attended, wo, targets, [[rows]] * 4, waits)

    def fan(a, b, c):
        return down(a), up(b), across(c)

    q0, kv0, other0 = ready(0, [low_rows, high_rows, far_rows], total0, [vmem(cache_sent)])
    total1 = second(1, [vmem(kv0)])
    attended0, pages0 = attend(0, q0, kv0, other0, [hbm(total1[0])])
    low, high = begin(attended0)
    q1, kv1, other1 = ready(1, [far_second], total1, [vmem(low)])
    low, high = down(low), up(high)
    a_, b_, c_ = next_three(attended0, [vmem(kv1)])
    a_ = down(a_)
    b_, c_ = add_up(
        [
            [(b_, 0, HERE), (high, cut, LINK)],
            [(c_, 0, HERE), (low, 0, LINK)],
        ],
        [vmem(other1)],
    )
    d_, e_, g_, own0 = last_four(attended0, [vmem(c_)])
    e_ = up(e_)
    b_, c_ = up(b_), across(c_)
    attended1, pages1 = attend(1, q1, kv1, other1, [hbm(own0)])
    me_there = lax.axis_index("segment").astype(jnp.int32)
    page = pages0.shape[1:]
    all_slots, half_slots = (sections,) + page, (sections // 2,) + page
    pages_each = pages0.shape[0]
    bits = [me_there // 2**k % 2 for k in range(4)]

    def first_trade(scalar_ref, ins, outs):
        slots, sent = outs
        for o in range(sections):
            slots[o] = jnp.zeros(page, BF)
        for p in range(blocks * pages_each):
            slots[scalar_ref[1 + p]] = ins[p // pages_each][p % pages_each]
        pick_sent(scalar_ref[0], slots, sent, 1, sections)

    def later_trade(before, step):
        def run(scalar_ref, ins, outs):
            merge_got(scalar_ref[0], ins[0], ins[1], outs[0], before, sections)
            pick_sent(scalar_ref[1], outs[0], outs[1], step, sections)

        return run

    def last_trade(scalar_ref, ins, outs):
        merge_got(scalar_ref[0], ins[0], ins[1], outs[0], 3, sections)

    def trade_with(sent, step):
        return lax.ppermute(sent, "segment", [(i, i ^ 1 << step) for i in range(sections)])

    low1, high1 = begin(attended1)
    a1, b1, c1 = next_three(attended1, [vmem(low1)])
    low1, high1 = down(low1), up(high1)
    trade = Trade(
        jnp.concatenate([bits[1][None], page_owner[0]]),
        [hbm(pages0), hbm(pages1)],
        [all_slots, half_slots],
        first_trade,
    )
    d_, g_, slots, sent = add_up(
        [[(d_, 0, HERE), (a_, 0, LINK), (c_, 0, LINK)], [(g_, 0, HERE), (b_, 0, LINK)]],
        [hbm(c1)],
        trade,
    )
    d_, g_ = down(d_), across(g_)
    got = trade_with(sent, 1)
    trade = Trade(
        jnp.stack([bits[1], bits[0]]),
        [hbm(slots), got],
        [all_slots, half_slots],
        later_trade(1, 0),
    )
    a1, b1, c1, slots, sent = add_up(
        [
            [(a1, 0, HERE)],
            [(b1, 0, HERE), (high1, cut, LOOSE)],
            [(c1, 0, HERE), (low1, 0, LOOSE)],
        ],
        [vmem(d_), vmem(g_)],
        trade,
    )
    a1, b1, c1 = fan(a1, b1, c1)
    got = trade_with(sent, 0)
    (done0,) = add_up(
        [[(rows_all, 0, 0), (own0, 0, HERE), (e_, 0, LINK), (d_, 0, LINK), (g_, 0, LINK)]]
    )
    first = lax.ppermute(done0, "segment", onward)
    d1, e1, g1, own1 = last_four(attended1, [vmem(done0)])
    e1 = up(e1)
    (next_hidden,) = put_block(None, [first], place, blocks)
    trade = Trade(
        jnp.stack([bits[0], bits[2]]),
        [hbm(slots), got],
        [all_slots, half_slots],
        later_trade(0, 2),
    )
    d1, g1, slots, sent = add_up(
        [[(d1, 0, HERE), (a1, 0, LINK), (c1, 0, LINK)], [(g1, 0, HERE), (b1, 0, LINK)]],
        [hbm(next_hidden)],
        trade,
    )
    d1, g1 = down(d1), across(g1)
    got = trade_with(sent, 2)
    slots, sent = trade_alone(
        Trade(
            jnp.stack([bits[2], bits[3]]),
            [hbm(slots), got],
            [all_slots, half_slots],
            later_trade(2, 3),
        ),
        (),
    )
    got = trade_with(sent, 3)
    done1 = add_up(
        [[(rows_all, 0, 1), (own1, 0, HERE), (e1, 0, LINK), (d1, 0, LINK), (g1, 0, LINK)]],
        [hbm(sent)],
    )
    last = [lax.ppermute(part, "segment", onward) for part in done1]
    (shipped,) = trade_alone(
        Trade(bits[3][None], [hbm(slots), got], [all_slots], last_trade), [vmem(done1[0])]
    )
    (next_hidden,) = put_block(next_hidden, last, 1 - place, blocks)
    return next_hidden[None], jnp.swapaxes(shipped, 2, 3)[None]


def solution(mesh):
    return jax.shard_map(
        local,
        mesh=mesh,
        in_specs=(
            P("segment", None, None, "tensor"),
            P("segment", None),
            P("segment", None, "tensor"),
            P("segment", "tensor"),
            P("segment", None, None, "tensor"),
            P("segment", None, "tensor"),
            P("segment", "tensor", None),
            P("segment", None, None, None, "tensor"),
            P("segment", None),
            P("segment", None),
            P("segment", None),
        ),
        out_specs=(P("segment", None, None, "tensor"), P("segment", None, None, None, "tensor")),
        check_vma=False,
    )
```

```python
import functools
import math

import jax
import jax.numpy as jnp
from jax import lax
from jax.experimental import pallas as pl
from jax.experimental.pallas import tpu as pltpu
from jax.sharding import PartitionSpec as P

HEAD_DIM = 128
LINK, LOOSE, HERE = "link", "loose", 0
LOWER, LENGTH = 8, 9
HALF = HEAD_DIM // 2
PAGE = 128
EPSILON = 1e-06
NZ = 4
TILE = 128
BF = jnp.bfloat16
F32 = jnp.float32

UP = [(y * NZ + z, y * NZ + (z + 1) % NZ) for y in range(2) for z in range(NZ)]
DOWN = [(y * NZ + z, y * NZ + (z - 1) % NZ) for y in range(2) for z in range(NZ)]
ACROSS = [(y * NZ + z, (1 - y) * NZ + z) for y in range(2) for z in range(NZ)]
MATE = [(i, i ^ 1) for i in range(2 * NZ)]

ANY = pl.BlockSpec(memory_space=pl.ANY)


def up(a):
    return lax.ppermute(a, "tensor", UP)


def down(a):
    return lax.ppermute(a, "tensor", DOWN)


def across(a):
    return lax.ppermute(a, "tensor", ACROSS)


def whole(shape):
    return pl.BlockSpec(shape, lambda *_: (0,) * len(shape))


def params(grid_dims=1, mebibytes=16):
    return pltpu.CompilerParams(
        vmem_limit_bytes=mebibytes * 1024 * 1024, dimension_semantics=("arbitrary",) * grid_dims
    )


def hbm(a):
    return pltpu.with_memory_space_constraint(a, pltpu.HBM)


def vmem(a):
    return pltpu.with_memory_space_constraint(a, pltpu.VMEM)


IN_VMEM = pl.BlockSpec(memory_space=pltpu.VMEM)
SMEM = pl.BlockSpec(memory_space=pltpu.SMEM)


def waits_on(waits):
    return [ANY] * len(waits)


def parked(shape, index=None):
    index = (0,) * len(shape) if index is None else index
    return pl.BlockSpec(shape, lambda *_: index, pipeline_mode=pl.Buffered(1))


def product_cost(rows, width, columns, count):
    return pl.CostEstimate(
        flops=2 * rows * width * columns * count,
        bytes_accessed=2 * width * (rows + columns) * count + 8 * rows * columns,
        transcendentals=0,
    )


NT = (((1,), (1,)), ((), ()))


def fold(squared):
    total = squared[:, :HEAD_DIM]
    for start in range(HEAD_DIM, squared.shape[1], HEAD_DIM):
        total = total + squared[:, start : start + HEAD_DIM]
    return total


def add_products(spots, shards, sources, gain, wq, wkv, total, waits=(), only=None):
    count = len(shards)
    blocks, rows, width = shards[0].shape
    place = (0, 0, 0)
    if only is not None:
        blocks, place = 1, (only, 0, 0)
    cols = wq.shape[1]
    fresh_cols = wkv.shape[0]
    first = total is None

    def pick(spot_ref, step):
        chosen = spot_ref[sources[0]]
        for j in range(1, count):
            chosen = jnp.where(step == j, spot_ref[sources[j]], chosen)
        return chosen

    ins = list(shards) + [hbm(gain), hbm(wq), hbm(wkv)]
    ins += ([] if first else [hbm(t) for t in total]) + list(waits)

    def kernel(src_ref, *refs):
        g_ref, wq_ref, wkv_ref = refs[count : count + 3]
        before, after = refs[count + 3 : count + 6], refs[-3:]
        for j in range(count):

            @pl.when(pl.program_id(0) == j)
            def _(j=j):
                x = refs[j][...].reshape(blocks * rows, width).astype(F32)
                scaled = (x * g_ref[...]).astype(BF)
                more = (
                    jnp.dot(scaled, wq_ref[...], preferred_element_type=F32),
                    lax.dot_general(scaled, wkv_ref[...], NT, preferred_element_type=F32),
                    fold(x * x),
                )
                for old, new, term in zip(after if j else before, after, more):
                    term = term.reshape(new.shape)
                    new[...] = term if j == 0 and first else old[...] + term

    shapes = [(blocks, rows, cols), (blocks, rows, fresh_cols), (blocks, rows, HEAD_DIM)]
    in_specs = [parked((blocks, rows, width), place)] * count + [
        pl.BlockSpec((1, width), lambda j, s: (0, pick(s, j))),
        pl.BlockSpec((width, cols), lambda j, s: (pick(s, j), 0)),
        pl.BlockSpec((fresh_cols, width), lambda j, s: (0, pick(s, j))),
    ]
    in_specs += [] if first else [parked(shape, place) for shape in shapes]
    in_specs += waits_on(waits)
    return pl.pallas_call(
        kernel,
        grid_spec=pltpu.PrefetchScalarGridSpec(
            num_scalar_prefetch=1,
            grid=(count,),
            in_specs=in_specs,
            out_specs=[parked(shape) for shape in shapes],
        ),
        out_shape=[pltpu.HBM(shape, F32) for shape in shapes],
        compiler_params=params(1, 32),
        cost_estimate=product_cost(blocks * rows, width, cols + fresh_cols, count),
        name="add_products",
    )(spots, *ins)


def finish_products(spots, block, pieces, source, gain, wq, wkv, total, qb, kvb, cosine, sine, waits=()):
    width = pieces[0].shape[1]
    sizes = [p.shape[0] for p in pieces]
    rows = sum(sizes)
    cols = wq.shape[1]
    fresh_cols = wkv.shape[0]
    half = fresh_cols // 2
    count = len(pieces)
    model = wq.shape[0]

    def kernel(src_ref, *refs):
        g_ref, wq_ref, wkv_ref, q_in, kv_in, sq_in, qb_ref, kvb_ref, cos_ref, sin_ref = refs[
            count : count + 10
        ]
        q_ref, kv_ref, send_ref, x_ref = refs[-4:]
        start = 0
        for piece, size in zip(refs[:count], sizes):
            x_ref[start : start + size] = piece[...]
            start += size
        x = x_ref[...].astype(F32)
        squares = jnp.sum(sq_in[...] + fold(x * x), axis=-1, keepdims=True)
        inverse = lax.rsqrt(squares / model + EPSILON)
        x_ref[...] = (x * g_ref[...]).astype(BF)
        scaled = x_ref[...]
        kv = kv_in[...] + lax.dot_general(scaled, wkv_ref[...], NT, preferred_element_type=F32)
        kv = (kv * inverse + kvb_ref[...]).T.reshape(2, half, rows)
        kv_ref[...] = kv
        send_ref[...] = kv.astype(BF)
        cos, sin = cos_ref[...], sin_ref[...]
        cos = jnp.concatenate([cos, cos], axis=0).T
        sin = jnp.concatenate([-sin, sin], axis=0).T
        for h in range(cols // HEAD_DIM):
            lanes = slice(h * HEAD_DIM, (h + 1) * HEAD_DIM)
            q = q_in[:, lanes] + jnp.dot(scaled, wq_ref[:, lanes], preferred_element_type=F32)
            q = q * inverse + qb_ref[:, lanes]
            q_ref[:, lanes] = (q * cos + pltpu.roll(q, HALF, 1) * sin).astype(BF)

    ins = [vmem(p) for p in pieces] + [hbm(gain), hbm(wq), hbm(wkv)]
    ins += [hbm(t) for t in total] + [qb, kvb, hbm(cosine), hbm(sine)]
    in_specs = [parked(p.shape) for p in pieces] + [
        pl.BlockSpec((1, width), lambda j, s: (0, s[source])),
        pl.BlockSpec((width, cols), lambda j, s: (s[source], 0)),
        pl.BlockSpec((fresh_cols, width), lambda j, s: (0, s[source])),
    ]
    in_specs += [
        pl.BlockSpec((None,) + t.shape[1:], lambda j, s: (0, 0, 0)) for t in total
    ]
    in_specs += [whole(qb.shape), whole(kvb.shape)]
    in_specs += [
        pl.BlockSpec((None,) + t.shape[1:], lambda j, s: (block, 0, 0)) for t in (cosine, sine)
    ]
    in_specs += waits_on(waits)
    return pl.pallas_call(
        kernel,
        grid_spec=pltpu.PrefetchScalarGridSpec(
            num_scalar_prefetch=1,
            grid=(1,),
            in_specs=in_specs,
            out_specs=[whole((rows, cols)), whole((2, half, rows)), whole((2, half, rows))],
            scratch_shapes=[pltpu.VMEM((rows, width), BF)],
        ),
        out_shape=[
            pltpu.VMEM((rows, cols), BF),
            pltpu.VMEM((2, half, rows), F32),
            pltpu.VMEM((2, half, rows), BF),
        ],
        compiler_params=params(),
        cost_estimate=product_cost(rows, width, cols + fresh_cols, 1),
        name="finish_products",
    )(spots, *ins, *waits)


def cut_out(parts, waits=()):
    def kernel(*refs):
        for i in range(len(parts)):
            refs[len(parts) + len(waits) + i][...] = refs[i][...]

    shapes = [
        a.shape if lead is None else a.shape[1:-2] + (size, a.shape[-1])
        for a, lead, _, size in parts
    ]
    in_specs = [
        whole(shape)
        if lead is None
        else pl.BlockSpec(
            (None,) + shape,
            functools.partial(lambda at, _: at, (lead,) + (0,) * (a.ndim - 3) + (nth, 0)),
        )
        for (a, lead, nth, _), shape in zip(parts, shapes)
    ]
    return pl.pallas_call(
        kernel,
        grid=(1,),
        in_specs=in_specs + waits_on(waits),
        out_specs=[whole(shape) for shape in shapes],
        out_shape=[pltpu.VMEM(shape, BF) for shape in shapes],
        compiler_params=params(),
        cost_estimate=pl.CostEstimate(
            flops=0, bytes_accessed=sum(4 * math.prod(s) for s in shapes), transcendentals=0
        ),
        name="cut_out",
    )(*[a for a, *_ in parts], *waits)


class Trade:
    def __init__(self, scalars, ins, outs, run):
        self.scalars, self.ins, self.outs, self.run = scalars, ins, outs, run


def slots_for(trade_step, sections):
    bit = 1 << trade_step
    return [
        (s, s // bit % 2, s // (2 * bit) * bit + s % bit) for s in range(sections)
    ]


def pick_sent(high, slots, out, step, sections):
    for mine in range(2):

        @pl.when(high == mine)
        def _(mine=mine):
            for s, side, place in slots_for(step, sections):
                if side != mine:
                    out[place] = slots[s]


def merge_got(high, slots, got, out, step, sections):
    for mine in range(2):

        @pl.when(high == mine)
        def _(mine=mine):
            for s, side, place in slots_for(step, sections):
                out[s] = slots[s] if side == mine else got[place]


def add_up(groups, waits=(), trade=None, halves=1):
    flat = [member for group in groups for member in group]
    extra_ins = [] if trade is None else trade.ins
    extra_outs = [] if trade is None else trade.outs
    scalars = jnp.zeros((1,), jnp.int32) if trade is None else trade.scalars

    def rows_of(array):
        return array.shape[-2]

    def kernel(scalar_ref, *refs):
        extra_refs = refs[len(flat) : len(flat) + len(extra_ins)]
        out_refs = refs[len(flat) + len(extra_ins) + len(waits) :]
        at = 0
        for nth, group in enumerate(groups):
            members = refs[at : at + len(group)]
            at += len(group)
            rows = rows_of(group[0][0])
            part = rows // halves
            marks = sorted(
                {0, part, rows} | {f for _, f, _ in group} | {f + rows_of(a) for a, f, _ in group}
            )
            for low, high in zip(marks, marks[1:]):
                total = None
                for ref, (array, first, _) in zip(members, group):
                    if first <= low and high <= first + rows_of(array):
                        term = ref[low - first : high - first].astype(F32)
                        total = term if total is None else total + term
                out = out_refs[nth * halves + low // part]
                out[low % part : low % part + high - low] = total.astype(BF)
        if trade is not None:
            trade.run(scalar_ref, extra_refs, out_refs[len(sums) :])

    def spec(array, kind):
        if kind is LINK:
            return IN_VMEM
        if array.ndim == 3:
            return pl.BlockSpec((None,) + array.shape[1:], lambda *_: (kind, 0, 0))
        return whole(array.shape)

    def placed(array, kind):
        return vmem(array) if kind is LINK else array if kind is LOOSE else hbm(array)

    sums = [
        (rows_of(group[0][0]) // halves, group[0][0].shape[-1])
        for group in groups
        for _ in range(halves)
    ]
    return pl.pallas_call(
        kernel,
        grid=(1,),
        in_specs=[SMEM]
        + [spec(a, kind) for a, _, kind in flat]
        + [whole(a.shape) for a in extra_ins]
        + waits_on(waits),
        out_specs=[IN_VMEM] * len(sums) + [whole(shape) for shape in extra_outs],
        out_shape=[pltpu.VMEM(shape, BF) for shape in sums]
        + [pltpu.HBM(shape, BF) for shape in extra_outs],
        compiler_params=params(),
        cost_estimate=pl.CostEstimate(
            flops=sum(a.size for a, *_ in flat),
            bytes_accessed=2 * sum(a.size for a, *_ in flat),
            transcendentals=0,
        ),
        name="add_up",
    )(
        scalars,
        *[placed(a, kind) for a, _, kind in flat],
        *extra_ins,
        *waits,
    )


def attention(spots, block, q, kv, other, cache, cache_other, cosine, sine, waits=()):
    rows, cols = q.shape
    half = kv.shape[1]
    resident = cache.shape[3]
    heads = cols // HEAD_DIM
    factor = math.log2(math.e) / math.sqrt(HEAD_DIM)

    def kernel(flag_ref, q_ref, kv_ref, other_ref, cache_ref, mate_ref, cos_ref, sin_ref, *rest):
        out_ref, page_ref, kt, vt, kf, vf = rest[len(waits) :]
        low = flag_ref[LOWER] == 1
        cos, sin = cos_ref[...], sin_ref[...]
        mine, theirs = kv_ref[0], other_ref[0].astype(F32)
        first, second = jnp.where(low, mine, theirs), jnp.where(low, theirs, mine)
        key_first = (first * cos - second * sin).astype(BF)
        key_second = (second * cos + first * sin).astype(BF)
        kf[:half], kf[half:] = key_first, key_second
        value, value_other = kv_ref[1].astype(BF), other_ref[1]
        pages = rows // PAGE
        for p in range(pages):
            page_ref[p, 1] = value[:, p * PAGE : (p + 1) * PAGE]

        @pl.when(low)
        def _():
            for p in range(pages):
                page_ref[p, 0] = key_first[:, p * PAGE : (p + 1) * PAGE]
            vf[:half], vf[half:] = value, value_other
            kt[:half], kt[half:] = cache_ref[0], mate_ref[0]
            vt[:half], vt[half:] = cache_ref[1], mate_ref[1]

        @pl.when(jnp.logical_not(low))
        def _():
            for p in range(pages):
                page_ref[p, 0] = key_second[:, p * PAGE : (p + 1) * PAGE]
            vf[:half], vf[half:] = value_other, value
            kt[:half], kt[half:] = mate_ref[0], cache_ref[0]
            vt[:half], vt[half:] = mate_ref[1], cache_ref[1]

        seen = lax.broadcasted_iota(jnp.int32, (1, resident), 1) < flag_ref[LENGTH + block]
        shut = jnp.where(seen, 0.0, -1e30).astype(F32)
        causal = lax.broadcasted_iota(jnp.int32, (TILE, TILE), 1) <= lax.broadcasted_iota(
            jnp.int32, (TILE, TILE), 0
        )
        nt = (((1,), (1,)), ((), ()))
        for r in range(rows // TILE):
            span = slice(r * TILE, (r + 1) * TILE)
            for h in range(heads):
                lanes = slice(h * HEAD_DIM, (h + 1) * HEAD_DIM)
                qh = q_ref[span, lanes]
                s_old = jnp.dot(qh, kt[...], preferred_element_type=F32) * factor + shut
                s_new = jnp.dot(qh, kf[:, : (r + 1) * TILE], preferred_element_type=F32) * factor
                s_diag = jnp.where(causal, s_new[:, r * TILE :], -1e30)
                peak = jnp.maximum(
                    jnp.max(s_old, axis=-1, keepdims=True), jnp.max(s_diag, axis=-1, keepdims=True)
                )
                if r:
                    s_past = s_new[:, : r * TILE]
                    peak = jnp.maximum(peak, jnp.max(s_past, axis=-1, keepdims=True))
                    p_past = jnp.exp2(s_past - peak)
                p_old, p_diag = jnp.exp2(s_old - peak), jnp.exp2(s_diag - peak)
                weight = jnp.sum(p_old, axis=-1, keepdims=True) + jnp.sum(
                    p_diag, axis=-1, keepdims=True
                )
                o = lax.dot_general(p_old.astype(BF), vt[...], nt, preferred_element_type=F32)
                o += lax.dot_general(
                    p_diag.astype(BF), vf[:, span], nt, preferred_element_type=F32
                )
                if r:
                    weight += jnp.sum(p_past, axis=-1, keepdims=True)
                    o += lax.dot_general(
                        p_past.astype(BF), vf[:, : r * TILE], nt, preferred_element_type=F32
                    )
                out_ref[span, lanes] = (o / weight).astype(BF)

    ins = [vmem(q), vmem(kv), vmem(other), hbm(cache), vmem(cache_other), hbm(cosine), hbm(sine)]
    per_block = lambda t: pl.BlockSpec((None,) + t.shape[1:], lambda *_: (block,) + (0,) * (t.ndim - 1))
    pairs = heads * rows * (resident + rows // 2 + TILE // 2)
    return pl.pallas_call(
        kernel,
        grid_spec=pltpu.PrefetchScalarGridSpec(
            num_scalar_prefetch=1,
            grid=(1,),
            in_specs=[whole(a.shape) for a in ins[:3]]
            + [per_block(a) for a in ins[3:]]
            + waits_on(waits),
            out_specs=[whole((rows, cols)), whole((rows // PAGE, 2, half, PAGE))],
            scratch_shapes=[
                pltpu.VMEM((HEAD_DIM, resident), BF),
                pltpu.VMEM((HEAD_DIM, resident), BF),
                pltpu.VMEM((HEAD_DIM, rows), BF),
                pltpu.VMEM((HEAD_DIM, rows), BF),
            ],
        ),
        out_shape=[
            pltpu.VMEM((rows, cols), BF),
            pltpu.HBM((rows // PAGE, 2, half, PAGE), BF),
        ],
        compiler_params=params(),
        cost_estimate=pl.CostEstimate(
            flops=8 * pairs * HEAD_DIM, bytes_accessed=4 * rows * cols, transcendentals=2 * pairs
        ),
        name="attention",
    )(spots, *ins, *waits)


def project(spots, attended, wo, targets, cuts, waits=(), send=False):
    rows, depth = attended.shape
    width = wo.shape[1] // (2 * NZ)
    count = len(targets)
    outs = [(size, width) for cut in cuts for size in cut]

    def kernel(spot_ref, w_ref, a_ref, *refs):
        out_refs, rest = refs[len(waits) : len(waits) + len(outs)], refs[len(waits) + len(outs) :]
        w_buf, sems = rest[:2]
        copies = []
        for j in range(count):
            span = pl.ds(pl.multiple_of(spot_ref[targets[j]] * width, width), width)
            copies.append(pltpu.make_async_copy(w_ref.at[:, span], w_buf.at[j], sems.at[j]))
            copies[j].start()
        nth, leaving = 0, []
        for j in range(count):
            copies[j].wait()
            start = 0
            for size in cuts[j]:
                share = jnp.dot(
                    a_ref[start : start + size], w_buf[j], preferred_element_type=F32
                ).astype(BF)
                if send:
                    out_refs[nth][...] = share
                else:
                    rest[2][nth] = share
                    leaving.append(
                        pltpu.make_async_copy(rest[2].at[nth], out_refs[nth], rest[3].at[nth])
                    )
                    leaving[nth].start()
                start += size
                nth += 1
        for copy in leaving:
            copy.wait()

    scratch = [pltpu.VMEM((count, depth, width), BF), pltpu.SemaphoreType.DMA((count,))]
    if not send:
        scratch += [pltpu.VMEM((count, rows, width), BF), pltpu.SemaphoreType.DMA((count,))]
    return pl.pallas_call(
        kernel,
        in_specs=[SMEM, ANY, IN_VMEM] + waits_on(waits),
        out_specs=[IN_VMEM if send else ANY] * len(outs),
        out_shape=[(pltpu.VMEM if send else pltpu.HBM)(o, BF) for o in outs],
        scratch_shapes=scratch,
        compiler_params=pltpu.CompilerParams(vmem_limit_bytes=16 * 1024 * 1024),
        cost_estimate=product_cost(rows, depth, width, count),
        name="project",
    )(spots, hbm(wo), vmem(attended), *waits)


def tables(places, row_count):
    position = places.astype(F32)[:, None] + jnp.arange(row_count, dtype=F32)
    frequency = jnp.exp(jnp.arange(HALF, dtype=F32) * (-2.0 * math.log(1000000.0) / HEAD_DIM))
    angles = frequency[None, :, None] * position[:, None, :]
    return jnp.cos(angles), jnp.sin(angles)


def put_block(into, parts, place, blocks):
    old = [] if into is None else [hbm(into)]
    size = parts[0].shape[0]
    shape = (size * len(parts), parts[0].shape[1])

    def kernel(place_ref, *refs):
        for i in range(len(parts)):
            refs[-1][i * size : (i + 1) * size] = refs[i][...]

    return pl.pallas_call(
        kernel,
        grid_spec=pltpu.PrefetchScalarGridSpec(
            num_scalar_prefetch=1,
            grid=(1,),
            in_specs=[IN_VMEM] * len(parts) + waits_on(old),
            out_specs=[pl.BlockSpec((None,) + shape, lambda _, p: (p[0], 0, 0))],
        ),
        out_shape=[pltpu.HBM((blocks,) + shape, BF)],
        input_output_aliases={1 + len(parts): 0} if old else {},
        compiler_params=params(),
        cost_estimate=pl.CostEstimate(
            flops=0, bytes_accessed=4 * math.prod(shape), transcendentals=0
        ),
        name="put_block",
    )(place[None], *[vmem(p) for p in parts], *old)


def trade_alone(trade, waits):
    def kernel(scalar_ref, *refs):
        trade.run(scalar_ref, refs[: len(trade.ins)], refs[len(trade.ins) + len(waits) :])

    return pl.pallas_call(
        kernel,
        in_specs=[SMEM] + [IN_VMEM] * len(trade.ins) + waits_on(waits),
        out_specs=[IN_VMEM] * len(trade.outs),
        out_shape=[pltpu.HBM(shape, BF) for shape in trade.outs],
        compiler_params=pltpu.CompilerParams(vmem_limit_bytes=16 * 1024 * 1024),
        cost_estimate=pl.CostEstimate(flops=0, bytes_accessed=2**20, transcendentals=0),
        name="trade_pages",
    )(trade.scalars, *trade.ins, *waits)


def local(
    hidden,
    norm_gain,
    query_weight,
    query_bias,
    key_value_weight,
    key_value_bias,
    output_weight,
    resident_cache,
    resident_length,
    plan,
    page_owner,
):
    rows_all = hidden[0]
    blocks, rows, width = rows_all.shape
    wq, wo = query_weight[0], output_weight[0]
    half = key_value_weight.shape[3]
    wkv = jnp.swapaxes(key_value_weight[0], 1, 2).reshape(2 * half, -1)
    me = lax.axis_index("tensor")
    y, z = me // NZ, me % NZ
    lower = z % 2 == 0
    sections = lax.axis_size("segment")
    onward = [(i, (i + 1) % sections) for i in range(sections)]

    def at(flip, shift):
        return flip * NZ + shift % NZ

    spots = jnp.concatenate(
        [
            jnp.stack([(y + f) % 2 * NZ + (z + d) % NZ for f in range(2) for d in range(NZ)]),
            lower.astype(jnp.int32)[None],
            resident_length[0],
        ]
    ).astype(jnp.int32)

    gain = norm_gain.astype(F32)
    qb = query_bias.astype(F32)
    kvb = key_value_bias.astype(F32).reshape(1, 2 * half)
    cosine, sine = tables(resident_length[0], rows)
    caches = jnp.swapaxes(resident_cache[0], 2, 3)

    plan_before = lax.ppermute(plan[0], "segment", onward)
    place = (plan_before[0] != 0).astype(jnp.int32)

    from_below, from_across, from_above = up(rows_all), across(rows_all), down(rows_all)
    far, diag_down, diag_up = up(from_below), across(from_below), down(from_across)
    total = add_products(
        spots,
        [hbm(rows_all), from_below, from_across, from_above],
        [at(0, 0), at(0, -1), at(1, 0), at(0, 1)],
        gain,
        wq,
        wkv,
        None,
        (hbm(cosine), hbm(sine), hbm(plan_before)),
    )
    quarter, cut = rows // 4, rows // 2
    low_rows, high_rows, far_rows = cut_out(
        [(diag_down, 0, 0, quarter), (diag_up, 0, 1, quarter), (far, 0, 1, cut)], [hbm(total[0])]
    )

    def mate(a):
        return lax.ppermute(a, "tensor", MATE)

    def second(b, waits):
        return add_products(
            spots,
            [far, diag_down, diag_up],
            [at(0, 2), at(1, -1), at(1, 1)],
            gain,
            wq,
            wkv,
            total,
            waits,
            b,
        )

    total0 = second(0, [vmem(low_rows)])
    low_rows, high_rows, far_rows = up(low_rows), down(high_rows), across(far_rows)
    far_second, cache_other = cut_out(
        [(far, 1, 0, rows), (hbm(caches), None, 0, 0)],
        [vmem(low_rows), vmem(high_rows), hbm(total0[0])],
    )
    cache_sent = cache_other
    cache_other, far_second = mate(cache_other), across(far_second)

    def ready(b, last, total, waits):
        q, kv, send = finish_products(
            spots, b, last, at(1, 2), gain, wq, wkv, total, qb, kvb, cosine, sine, waits
        )
        return q, kv, mate(send)

    def attend(b, q, kv, other, waits):
        return attention(
            spots, b, q, kv, other, caches, cache_other, cosine, sine, waits
        )

    def begin(attended, first_rows):
        parts = [first_rows, rows - first_rows]
        return project(spots, attended, wo, [at(1, 2)], [parts], send=True)

    def next_three(attended, waits):
        targets = [at(0, 2), at(1, 1), at(1, -1)]
        return project(spots, attended, wo, targets, [[rows]] * 3, waits)

    def last_four(attended, waits):
        targets = [at(0, -1), at(0, 1), at(1, 0), at(0, 0)]
        return project(spots, attended, wo, targets, [[rows]] * 4, waits)

    def fan(a, b, c):
        return down(a), up(b), across(c)

    q0, kv0, other0 = ready(0, [low_rows, high_rows, far_rows], total0, [vmem(cache_sent)])
    total1 = second(1, [vmem(kv0)])
    attended0, pages0 = attend(0, q0, kv0, other0, [hbm(total1[0])])
    low, high = begin(attended0, cut)
    q1, kv1, other1 = ready(1, [far_second], total1, [vmem(low)])
    low, high = down(low), up(high)
    a_, b_, c_ = next_three(attended0, [vmem(kv1)])
    a_ = down(a_)
    b_, c_ = add_up(
        [
            [(b_, 0, HERE), (high, cut, LINK)],
            [(c_, 0, HERE), (low, 0, LINK)],
        ],
        [vmem(other1)],
    )
    d_, e_, g_, own0 = last_four(attended0, [vmem(c_)])
    e_ = up(e_)
    b_, c_ = up(b_), across(c_)
    attended1, pages1 = attend(1, q1, kv1, other1, [hbm(own0)])
    me_there = lax.axis_index("segment").astype(jnp.int32)
    page = pages0.shape[1:]
    all_slots, half_slots = (sections,) + page, (sections // 2,) + page
    pages_each = pages0.shape[0]
    bits = [me_there // 2**k % 2 for k in range(4)]

    def first_trade(scalar_ref, ins, outs):
        slots, sent = outs
        for o in range(sections):
            slots[o] = jnp.zeros(page, BF)
        for p in range(blocks * pages_each):
            slots[scalar_ref[1 + p]] = ins[p // pages_each][p % pages_each]
        pick_sent(scalar_ref[0], slots, sent, 1, sections)

    def later_trade(before, step):
        def run(scalar_ref, ins, outs):
            merge_got(scalar_ref[0], ins[0], ins[1], outs[0], before, sections)
            pick_sent(scalar_ref[1], outs[0], outs[1], step, sections)

        return run

    def last_trade(scalar_ref, ins, outs):
        merge_got(scalar_ref[0], ins[0], ins[1], outs[0], 3, sections)

    def trade_with(sent, step):
        return lax.ppermute(sent, "segment", [(i, i ^ 1 << step) for i in range(sections)])

    fewer = rows // 3
    low1, high1 = begin(attended1, fewer)
    trade = Trade(
        jnp.concatenate([bits[1][None], page_owner[0]]),
        [hbm(pages0), hbm(pages1)],
        [all_slots, half_slots],
        first_trade,
    )
    d_, g_, slots, sent = add_up(
        [[(d_, 0, HERE), (a_, 0, LINK), (c_, 0, LINK)], [(g_, 0, HERE), (b_, 0, LINK)]],
        [vmem(low1)],
        trade,
    )
    low1, high1 = down(low1), up(high1)
    d_, g_ = down(d_), across(g_)
    got = trade_with(sent, 1)
    a1, b1, c1 = next_three(attended1, [vmem(e_)])
    trade = Trade(
        jnp.stack([bits[1], bits[0]]),
        [hbm(slots), got],
        [all_slots, half_slots],
        later_trade(1, 0),
    )
    a1, b1, c1, done0, slots, sent = add_up(
        [
            [(a1, 0, HERE)],
            [(b1, 0, HERE), (high1, fewer, LOOSE)],
            [(c1, 0, HERE), (low1, 0, LOOSE)],
            [(rows_all, 0, 0), (own0, 0, HERE), (e_, 0, LINK), (d_, 0, LINK), (g_, 0, LINK)],
        ],
        (),
        trade,
    )
    a1, b1, c1 = fan(a1, b1, c1)
    first = lax.ppermute(done0, "segment", onward)
    got = trade_with(sent, 0)
    d1, e1, g1, own1 = last_four(attended1, [got])
    e1 = up(e1)
    (next_hidden,) = put_block(None, [first], place, blocks)
    slots, sent = trade_alone(
        Trade(
            jnp.stack([bits[0], bits[2]]),
            [hbm(slots), got],
            [all_slots, half_slots],
            later_trade(0, 2),
        ),
        [hbm(own1)],
    )
    d1, g1 = add_up(
        [[(d1, 0, HERE), (a1, 0, LINK), (c1, 0, LINK)], [(g1, 0, HERE), (b1, 0, LINK)]],
        [hbm(next_hidden), hbm(sent)],
    )
    d1, g1 = down(d1), across(g1)
    got = trade_with(sent, 2)
    slots, sent = trade_alone(
        Trade(
            jnp.stack([bits[2], bits[3]]),
            [hbm(slots), got],
            [all_slots, half_slots],
            later_trade(2, 3),
        ),
        (),
    )
    got = trade_with(sent, 3)
    done1 = add_up(
        [[(rows_all, 0, 1), (own1, 0, HERE), (e1, 0, LINK), (d1, 0, LINK), (g1, 0, LINK)]],
        [hbm(sent)],
    )
    last = [lax.ppermute(part, "segment", onward) for part in done1]
    (shipped,) = trade_alone(
        Trade(bits[3][None], [hbm(slots), got], [all_slots], last_trade), [vmem(done1[0])]
    )
    (next_hidden,) = put_block(next_hidden, last, 1 - place, blocks)
    return next_hidden[None], jnp.swapaxes(shipped, 2, 3)[None]


def solution(mesh):
    return jax.shard_map(
        local,
        mesh=mesh,
        in_specs=(
            P("segment", None, None, "tensor"),
            P("segment", None),
            P("segment", None, "tensor"),
            P("segment", "tensor"),
            P("segment", None, None, "tensor"),
            P("segment", None, "tensor"),
            P("segment", "tensor", None),
            P("segment", None, None, None, "tensor"),
            P("segment", None),
            P("segment", None),
            P("segment", None),
        ),
        out_specs=(P("segment", None, None, "tensor"), P("segment", None, None, None, "tensor")),
        check_vma=False,
    )
```

```python
import functools
import math

import jax
import jax.numpy as jnp
from jax import lax
from jax.experimental import pallas as pl
from jax.experimental.pallas import tpu as pltpu
from jax.sharding import PartitionSpec as P

HEAD_DIM = 128
LINK, LOOSE, HERE = "link", "loose", 0
LOWER, LENGTH = 8, 9
HALF = HEAD_DIM // 2
PAGE = 128
EPSILON = 1e-06
NZ = 4
TILE = 128
BF = jnp.bfloat16
F32 = jnp.float32

UP = [(y * NZ + z, y * NZ + (z + 1) % NZ) for y in range(2) for z in range(NZ)]
DOWN = [(y * NZ + z, y * NZ + (z - 1) % NZ) for y in range(2) for z in range(NZ)]
ACROSS = [(y * NZ + z, (1 - y) * NZ + z) for y in range(2) for z in range(NZ)]
MATE = [(i, i ^ 1) for i in range(2 * NZ)]

ANY = pl.BlockSpec(memory_space=pl.ANY)


def up(a):
    return lax.ppermute(a, "tensor", UP)


def down(a):
    return lax.ppermute(a, "tensor", DOWN)


def across(a):
    return lax.ppermute(a, "tensor", ACROSS)


def whole(shape):
    return pl.BlockSpec(shape, lambda *_: (0,) * len(shape))


def params(grid_dims=1, mebibytes=16):
    return pltpu.CompilerParams(
        vmem_limit_bytes=mebibytes * 1024 * 1024, dimension_semantics=("arbitrary",) * grid_dims
    )


def hbm(a):
    return pltpu.with_memory_space_constraint(a, pltpu.HBM)


def vmem(a):
    return pltpu.with_memory_space_constraint(a, pltpu.VMEM)


IN_VMEM = pl.BlockSpec(memory_space=pltpu.VMEM)
SMEM = pl.BlockSpec(memory_space=pltpu.SMEM)


def waits_on(waits):
    return [ANY] * len(waits)


def parked(shape, index=None):
    index = (0,) * len(shape) if index is None else index
    return pl.BlockSpec(shape, lambda *_: index, pipeline_mode=pl.Buffered(1))


def product_cost(rows, width, columns, count):
    return pl.CostEstimate(
        flops=2 * rows * width * columns * count,
        bytes_accessed=2 * width * (rows + columns) * count + 8 * rows * columns,
        transcendentals=0,
    )


NT = (((1,), (1,)), ((), ()))


def fold(squared):
    total = squared[:, :HEAD_DIM]
    for start in range(HEAD_DIM, squared.shape[1], HEAD_DIM):
        total = total + squared[:, start : start + HEAD_DIM]
    return total


def add_products(spots, shards, sources, gain, wq, wkv, total, waits=(), only=None):
    count = len(shards)
    blocks, rows, width = shards[0].shape
    place = (0, 0, 0)
    if only is not None:
        blocks, place = 1, (only, 0, 0)
    cols = wq.shape[1]
    fresh_cols = wkv.shape[0]
    first = total is None

    def pick(spot_ref, step):
        chosen = spot_ref[sources[0]]
        for j in range(1, count):
            chosen = jnp.where(step == j, spot_ref[sources[j]], chosen)
        return chosen

    ins = list(shards) + [hbm(gain), hbm(wq), hbm(wkv)]
    ins += ([] if first else [hbm(t) for t in total]) + list(waits)

    def kernel(src_ref, *refs):
        g_ref, wq_ref, wkv_ref = refs[count : count + 3]
        before, after = refs[count + 3 : count + 6], refs[-3:]
        for j in range(count):

            @pl.when(pl.program_id(0) == j)
            def _(j=j):
                x = refs[j][...].reshape(blocks * rows, width).astype(F32)
                scaled = (x * g_ref[...]).astype(BF)
                more = (
                    jnp.dot(scaled, wq_ref[...], preferred_element_type=F32),
                    lax.dot_general(scaled, wkv_ref[...], NT, preferred_element_type=F32),
                    fold(x * x),
                )
                for old, new, term in zip(after if j else before, after, more):
                    term = term.reshape(new.shape)
                    new[...] = term if j == 0 and first else old[...] + term

    shapes = [(blocks, rows, cols), (blocks, rows, fresh_cols), (blocks, rows, HEAD_DIM)]
    in_specs = [parked((blocks, rows, width), place)] * count + [
        pl.BlockSpec((1, width), lambda j, s: (0, pick(s, j))),
        pl.BlockSpec((width, cols), lambda j, s: (pick(s, j), 0)),
        pl.BlockSpec((fresh_cols, width), lambda j, s: (0, pick(s, j))),
    ]
    in_specs += [] if first else [parked(shape, place) for shape in shapes]
    in_specs += waits_on(waits)
    return pl.pallas_call(
        kernel,
        grid_spec=pltpu.PrefetchScalarGridSpec(
            num_scalar_prefetch=1,
            grid=(count,),
            in_specs=in_specs,
            out_specs=[parked(shape) for shape in shapes],
        ),
        out_shape=[pltpu.HBM(shape, F32) for shape in shapes],
        compiler_params=params(1, 32),
        cost_estimate=product_cost(blocks * rows, width, cols + fresh_cols, count),
        name="add_products",
    )(spots, *ins)


def finish_products(spots, block, pieces, source, gain, wq, wkv, total, qb, kvb, cosine, sine, waits=()):
    width = pieces[0].shape[1]
    sizes = [p.shape[0] for p in pieces]
    rows = sum(sizes)
    cols = wq.shape[1]
    fresh_cols = wkv.shape[0]
    half = fresh_cols // 2
    count = len(pieces)
    model = wq.shape[0]

    def kernel(src_ref, *refs):
        g_ref, wq_ref, wkv_ref, q_in, kv_in, sq_in, qb_ref, kvb_ref, cos_ref, sin_ref = refs[
            count : count + 10
        ]
        q_ref, kv_ref, send_ref, x_ref = refs[-4:]
        start = 0
        for piece, size in zip(refs[:count], sizes):
            x_ref[start : start + size] = piece[...]
            start += size
        x = x_ref[...].astype(F32)
        squares = jnp.sum(sq_in[...] + fold(x * x), axis=-1, keepdims=True)
        inverse = lax.rsqrt(squares / model + EPSILON)
        x_ref[...] = (x * g_ref[...]).astype(BF)
        scaled = x_ref[...]
        kv = kv_in[...] + lax.dot_general(scaled, wkv_ref[...], NT, preferred_element_type=F32)
        kv = (kv * inverse + kvb_ref[...]).T.reshape(2, half, rows)
        kv_ref[...] = kv
        send_ref[...] = kv.astype(BF)
        cos, sin = cos_ref[...], sin_ref[...]
        cos = jnp.concatenate([cos, cos], axis=0).T
        sin = jnp.concatenate([-sin, sin], axis=0).T
        for h in range(cols // HEAD_DIM):
            lanes = slice(h * HEAD_DIM, (h + 1) * HEAD_DIM)
            q = q_in[:, lanes] + jnp.dot(scaled, wq_ref[:, lanes], preferred_element_type=F32)
            q = q * inverse + qb_ref[:, lanes]
            q_ref[:, lanes] = (q * cos + pltpu.roll(q, HALF, 1) * sin).astype(BF)

    ins = [vmem(p) for p in pieces] + [hbm(gain), hbm(wq), hbm(wkv)]
    ins += [hbm(t) for t in total] + [qb, kvb, hbm(cosine), hbm(sine)]
    in_specs = [parked(p.shape) for p in pieces] + [
        pl.BlockSpec((1, width), lambda j, s: (0, s[source])),
        pl.BlockSpec((width, cols), lambda j, s: (s[source], 0)),
        pl.BlockSpec((fresh_cols, width), lambda j, s: (0, s[source])),
    ]
    in_specs += [
        pl.BlockSpec((None,) + t.shape[1:], lambda j, s: (0, 0, 0)) for t in total
    ]
    in_specs += [whole(qb.shape), whole(kvb.shape)]
    in_specs += [
        pl.BlockSpec((None,) + t.shape[1:], lambda j, s: (block, 0, 0)) for t in (cosine, sine)
    ]
    in_specs += waits_on(waits)
    return pl.pallas_call(
        kernel,
        grid_spec=pltpu.PrefetchScalarGridSpec(
            num_scalar_prefetch=1,
            grid=(1,),
            in_specs=in_specs,
            out_specs=[whole((rows, cols)), whole((2, half, rows)), whole((2, half, rows))],
            scratch_shapes=[pltpu.VMEM((rows, width), BF)],
        ),
        out_shape=[
            pltpu.VMEM((rows, cols), BF),
            pltpu.VMEM((2, half, rows), F32),
            pltpu.VMEM((2, half, rows), BF),
        ],
        compiler_params=params(),
        cost_estimate=product_cost(rows, width, cols + fresh_cols, 1),
        name="finish_products",
    )(spots, *ins, *waits)


def cut_out(parts, waits=()):
    def kernel(*refs):
        for i in range(len(parts)):
            refs[len(parts) + len(waits) + i][...] = refs[i][...]

    shapes = [
        a.shape if lead is None else a.shape[1:-2] + (size, a.shape[-1])
        for a, lead, _, size in parts
    ]
    in_specs = [
        whole(shape)
        if lead is None
        else pl.BlockSpec(
            (None,) + shape,
            functools.partial(lambda at, _: at, (lead,) + (0,) * (a.ndim - 3) + (nth, 0)),
        )
        for (a, lead, nth, _), shape in zip(parts, shapes)
    ]
    return pl.pallas_call(
        kernel,
        grid=(1,),
        in_specs=in_specs + waits_on(waits),
        out_specs=[whole(shape) for shape in shapes],
        out_shape=[pltpu.VMEM(shape, BF) for shape in shapes],
        compiler_params=params(),
        cost_estimate=pl.CostEstimate(
            flops=0, bytes_accessed=sum(4 * math.prod(s) for s in shapes), transcendentals=0
        ),
        name="cut_out",
    )(*[a for a, *_ in parts], *waits)


class Trade:
    def __init__(self, scalars, ins, outs, run):
        self.scalars, self.ins, self.outs, self.run = scalars, ins, outs, run


def slots_for(trade_step, sections):
    bit = 1 << trade_step
    return [
        (s, s // bit % 2, s // (2 * bit) * bit + s % bit) for s in range(sections)
    ]


def pick_sent(high, slots, out, step, sections):
    for mine in range(2):

        @pl.when(high == mine)
        def _(mine=mine):
            for s, side, place in slots_for(step, sections):
                if side != mine:
                    out[place] = slots[s]


def merge_got(high, slots, got, out, step, sections):
    for mine in range(2):

        @pl.when(high == mine)
        def _(mine=mine):
            for s, side, place in slots_for(step, sections):
                out[s] = slots[s] if side == mine else got[place]


def add_up(groups, waits=(), trade=None, halves=1):
    flat = [member for group in groups for member in group]
    extra_ins = [] if trade is None else trade.ins
    extra_outs = [] if trade is None else trade.outs
    scalars = jnp.zeros((1,), jnp.int32) if trade is None else trade.scalars

    def rows_of(array):
        return array.shape[-2]

    def kernel(scalar_ref, *refs):
        extra_refs = refs[len(flat) : len(flat) + len(extra_ins)]
        out_refs = refs[len(flat) + len(extra_ins) + len(waits) :]
        at = 0
        for nth, group in enumerate(groups):
            members = refs[at : at + len(group)]
            at += len(group)
            rows = rows_of(group[0][0])
            part = rows // halves
            marks = sorted(
                {0, part, rows} | {f for _, f, _ in group} | {f + rows_of(a) for a, f, _ in group}
            )
            for low, high in zip(marks, marks[1:]):
                total = None
                for ref, (array, first, _) in zip(members, group):
                    if first <= low and high <= first + rows_of(array):
                        term = ref[low - first : high - first].astype(F32)
                        total = term if total is None else total + term
                out = out_refs[nth * halves + low // part]
                out[low % part : low % part + high - low] = total.astype(BF)
        if trade is not None:
            trade.run(scalar_ref, extra_refs, out_refs[len(sums) :])

    def spec(array, kind):
        if kind is LINK:
            return IN_VMEM
        if array.ndim == 3:
            return pl.BlockSpec((None,) + array.shape[1:], lambda *_: (kind, 0, 0))
        return whole(array.shape)

    def placed(array, kind):
        return vmem(array) if kind is LINK else array if kind is LOOSE else hbm(array)

    sums = [
        (rows_of(group[0][0]) // halves, group[0][0].shape[-1])
        for group in groups
        for _ in range(halves)
    ]
    return pl.pallas_call(
        kernel,
        grid=(1,),
        in_specs=[SMEM]
        + [spec(a, kind) for a, _, kind in flat]
        + [whole(a.shape) for a in extra_ins]
        + waits_on(waits),
        out_specs=[IN_VMEM] * len(sums) + [whole(shape) for shape in extra_outs],
        out_shape=[pltpu.VMEM(shape, BF) for shape in sums]
        + [pltpu.HBM(shape, BF) for shape in extra_outs],
        compiler_params=params(),
        cost_estimate=pl.CostEstimate(
            flops=sum(a.size for a, *_ in flat),
            bytes_accessed=2 * sum(a.size for a, *_ in flat),
            transcendentals=0,
        ),
        name="add_up",
    )(
        scalars,
        *[placed(a, kind) for a, _, kind in flat],
        *extra_ins,
        *waits,
    )


def attention(spots, block, q, kv, other, cache, cache_other, cosine, sine, waits=()):
    rows, cols = q.shape
    half = kv.shape[1]
    resident = cache.shape[3]
    heads = cols // HEAD_DIM
    factor = math.log2(math.e) / math.sqrt(HEAD_DIM)

    def kernel(flag_ref, q_ref, kv_ref, other_ref, cache_ref, mate_ref, cos_ref, sin_ref, *rest):
        out_ref, page_ref, kt, vt, kf, vf = rest[len(waits) :]
        low = flag_ref[LOWER] == 1
        cos, sin = cos_ref[...], sin_ref[...]
        mine, theirs = kv_ref[0], other_ref[0].astype(F32)
        first, second = jnp.where(low, mine, theirs), jnp.where(low, theirs, mine)
        key_first = (first * cos - second * sin).astype(BF)
        key_second = (second * cos + first * sin).astype(BF)
        kf[:half], kf[half:] = key_first, key_second
        value, value_other = kv_ref[1].astype(BF), other_ref[1]
        pages = rows // PAGE
        for p in range(pages):
            page_ref[p, 1] = value[:, p * PAGE : (p + 1) * PAGE]

        @pl.when(low)
        def _():
            for p in range(pages):
                page_ref[p, 0] = key_first[:, p * PAGE : (p + 1) * PAGE]
            vf[:half], vf[half:] = value, value_other
            kt[:half], kt[half:] = cache_ref[0], mate_ref[0]
            vt[:half], vt[half:] = cache_ref[1], mate_ref[1]

        @pl.when(jnp.logical_not(low))
        def _():
            for p in range(pages):
                page_ref[p, 0] = key_second[:, p * PAGE : (p + 1) * PAGE]
            vf[:half], vf[half:] = value_other, value
            kt[:half], kt[half:] = mate_ref[0], cache_ref[0]
            vt[:half], vt[half:] = mate_ref[1], cache_ref[1]

        seen = lax.broadcasted_iota(jnp.int32, (1, resident), 1) < flag_ref[LENGTH + block]
        shut = jnp.where(seen, 0.0, -1e30).astype(F32)
        causal = lax.broadcasted_iota(jnp.int32, (TILE, TILE), 1) <= lax.broadcasted_iota(
            jnp.int32, (TILE, TILE), 0
        )
        nt = (((1,), (1,)), ((), ()))
        for r in range(rows // TILE):
            span = slice(r * TILE, (r + 1) * TILE)
            for h in range(heads):
                lanes = slice(h * HEAD_DIM, (h + 1) * HEAD_DIM)
                qh = q_ref[span, lanes]
                s_old = jnp.dot(qh, kt[...], preferred_element_type=F32) * factor + shut
                s_new = jnp.dot(qh, kf[:, : (r + 1) * TILE], preferred_element_type=F32) * factor
                s_diag = jnp.where(causal, s_new[:, r * TILE :], -1e30)
                peak = jnp.maximum(
                    jnp.max(s_old, axis=-1, keepdims=True), jnp.max(s_diag, axis=-1, keepdims=True)
                )
                if r:
                    s_past = s_new[:, : r * TILE]
                    peak = jnp.maximum(peak, jnp.max(s_past, axis=-1, keepdims=True))
                    p_past = jnp.exp2(s_past - peak)
                p_old, p_diag = jnp.exp2(s_old - peak), jnp.exp2(s_diag - peak)
                weight = jnp.sum(p_old, axis=-1, keepdims=True) + jnp.sum(
                    p_diag, axis=-1, keepdims=True
                )
                o = lax.dot_general(p_old.astype(BF), vt[...], nt, preferred_element_type=F32)
                o += lax.dot_general(
                    p_diag.astype(BF), vf[:, span], nt, preferred_element_type=F32
                )
                if r:
                    weight += jnp.sum(p_past, axis=-1, keepdims=True)
                    o += lax.dot_general(
                        p_past.astype(BF), vf[:, : r * TILE], nt, preferred_element_type=F32
                    )
                out_ref[span, lanes] = (o / weight).astype(BF)

    ins = [vmem(q), vmem(kv), vmem(other), hbm(cache), vmem(cache_other), hbm(cosine), hbm(sine)]
    per_block = lambda t: pl.BlockSpec((None,) + t.shape[1:], lambda *_: (block,) + (0,) * (t.ndim - 1))
    pairs = heads * rows * (resident + rows // 2 + TILE // 2)
    return pl.pallas_call(
        kernel,
        grid_spec=pltpu.PrefetchScalarGridSpec(
            num_scalar_prefetch=1,
            grid=(1,),
            in_specs=[whole(a.shape) for a in ins[:3]]
            + [per_block(a) for a in ins[3:]]
            + waits_on(waits),
            out_specs=[whole((rows, cols)), whole((rows // PAGE, 2, half, PAGE))],
            scratch_shapes=[
                pltpu.VMEM((HEAD_DIM, resident), BF),
                pltpu.VMEM((HEAD_DIM, resident), BF),
                pltpu.VMEM((HEAD_DIM, rows), BF),
                pltpu.VMEM((HEAD_DIM, rows), BF),
            ],
        ),
        out_shape=[
            pltpu.VMEM((rows, cols), BF),
            pltpu.HBM((rows // PAGE, 2, half, PAGE), BF),
        ],
        compiler_params=params(),
        cost_estimate=pl.CostEstimate(
            flops=8 * pairs * HEAD_DIM, bytes_accessed=4 * rows * cols, transcendentals=2 * pairs
        ),
        name="attention",
    )(spots, *ins, *waits)


def project(spots, attended, wo, targets, cuts, waits=(), send=False):
    rows, depth = attended.shape
    width = wo.shape[1] // (2 * NZ)
    count = len(targets)
    outs = [(size, width) for cut in cuts for size in cut]

    def kernel(spot_ref, w_ref, a_ref, *refs):
        out_refs, rest = refs[len(waits) : len(waits) + len(outs)], refs[len(waits) + len(outs) :]
        w_buf, sems = rest[:2]
        copies = []
        for j in range(count):
            span = pl.ds(pl.multiple_of(spot_ref[targets[j]] * width, width), width)
            copies.append(pltpu.make_async_copy(w_ref.at[:, span], w_buf.at[j], sems.at[j]))
            copies[j].start()
        nth, leaving = 0, []
        for j in range(count):
            copies[j].wait()
            start = 0
            for size in cuts[j]:
                share = jnp.dot(
                    a_ref[start : start + size], w_buf[j], preferred_element_type=F32
                ).astype(BF)
                if send:
                    out_refs[nth][...] = share
                else:
                    rest[2][nth] = share
                    leaving.append(
                        pltpu.make_async_copy(rest[2].at[nth], out_refs[nth], rest[3].at[nth])
                    )
                    leaving[nth].start()
                start += size
                nth += 1
        for copy in leaving:
            copy.wait()

    scratch = [pltpu.VMEM((count, depth, width), BF), pltpu.SemaphoreType.DMA((count,))]
    if not send:
        scratch += [pltpu.VMEM((count, rows, width), BF), pltpu.SemaphoreType.DMA((count,))]
    return pl.pallas_call(
        kernel,
        in_specs=[SMEM, ANY, IN_VMEM] + waits_on(waits),
        out_specs=[IN_VMEM if send else ANY] * len(outs),
        out_shape=[(pltpu.VMEM if send else pltpu.HBM)(o, BF) for o in outs],
        scratch_shapes=scratch,
        compiler_params=pltpu.CompilerParams(vmem_limit_bytes=16 * 1024 * 1024),
        cost_estimate=product_cost(rows, depth, width, count),
        name="project",
    )(spots, hbm(wo), vmem(attended), *waits)


def tables(places, row_count):
    position = places.astype(F32)[:, None] + jnp.arange(row_count, dtype=F32)
    frequency = jnp.exp(jnp.arange(HALF, dtype=F32) * (-2.0 * math.log(1000000.0) / HEAD_DIM))
    angles = frequency[None, :, None] * position[:, None, :]
    return jnp.cos(angles), jnp.sin(angles)


def put_block(into, parts, place, blocks):
    old = [] if into is None else [hbm(into)]
    size = parts[0].shape[0]
    shape = (size * len(parts), parts[0].shape[1])

    def kernel(place_ref, *refs):
        for i in range(len(parts)):
            refs[-1][i * size : (i + 1) * size] = refs[i][...]

    return pl.pallas_call(
        kernel,
        grid_spec=pltpu.PrefetchScalarGridSpec(
            num_scalar_prefetch=1,
            grid=(1,),
            in_specs=[IN_VMEM] * len(parts) + waits_on(old),
            out_specs=[pl.BlockSpec((None,) + shape, lambda _, p: (p[0], 0, 0))],
        ),
        out_shape=[pltpu.HBM((blocks,) + shape, BF)],
        input_output_aliases={1 + len(parts): 0} if old else {},
        compiler_params=params(),
        cost_estimate=pl.CostEstimate(
            flops=0, bytes_accessed=4 * math.prod(shape), transcendentals=0
        ),
        name="put_block",
    )(place[None], *[vmem(p) for p in parts], *old)


def trade_alone(trade, waits):
    def kernel(scalar_ref, *refs):
        trade.run(scalar_ref, refs[: len(trade.ins)], refs[len(trade.ins) + len(waits) :])

    return pl.pallas_call(
        kernel,
        in_specs=[SMEM] + [IN_VMEM] * len(trade.ins) + waits_on(waits),
        out_specs=[IN_VMEM] * len(trade.outs),
        out_shape=[pltpu.HBM(shape, BF) for shape in trade.outs],
        compiler_params=pltpu.CompilerParams(vmem_limit_bytes=16 * 1024 * 1024),
        cost_estimate=pl.CostEstimate(flops=0, bytes_accessed=2**20, transcendentals=0),
        name="trade_pages",
    )(trade.scalars, *trade.ins, *waits)


def local(
    hidden,
    norm_gain,
    query_weight,
    query_bias,
    key_value_weight,
    key_value_bias,
    output_weight,
    resident_cache,
    resident_length,
    plan,
    page_owner,
):
    rows_all = hidden[0]
    blocks, rows, width = rows_all.shape
    wq, wo = query_weight[0], output_weight[0]
    half = key_value_weight.shape[3]
    wkv = jnp.swapaxes(key_value_weight[0], 1, 2).reshape(2 * half, -1)
    me = lax.axis_index("tensor")
    y, z = me // NZ, me % NZ
    lower = z % 2 == 0
    sections = lax.axis_size("segment")
    onward = [(i, (i + 1) % sections) for i in range(sections)]

    def at(flip, shift):
        return flip * NZ + shift % NZ

    spots = jnp.concatenate(
        [
            jnp.stack([(y + f) % 2 * NZ + (z + d) % NZ for f in range(2) for d in range(NZ)]),
            lower.astype(jnp.int32)[None],
            resident_length[0],
        ]
    ).astype(jnp.int32)

    gain = norm_gain.astype(F32)
    qb = query_bias.astype(F32)
    kvb = key_value_bias.astype(F32).reshape(1, 2 * half)
    cosine, sine = tables(resident_length[0], rows)
    caches = jnp.swapaxes(resident_cache[0], 2, 3)

    plan_before = lax.ppermute(plan[0], "segment", onward)
    place = (plan_before[0] != 0).astype(jnp.int32)

    from_below, from_across, from_above = up(rows_all), across(rows_all), down(rows_all)
    far, diag_down, diag_up = up(from_below), across(from_below), down(from_across)
    total = add_products(
        spots,
        [hbm(rows_all), from_below, from_across, from_above],
        [at(0, 0), at(0, -1), at(1, 0), at(0, 1)],
        gain,
        wq,
        wkv,
        None,
        (hbm(cosine), hbm(sine), hbm(plan_before)),
    )
    quarter, cut = rows // 4, rows // 2
    low_rows, high_rows, far_rows = cut_out(
        [(diag_down, 0, 0, quarter), (diag_up, 0, 1, quarter), (far, 0, 1, cut)], [hbm(total[0])]
    )

    def mate(a):
        return lax.ppermute(a, "tensor", MATE)

    def second(b, waits):
        return add_products(
            spots,
            [far, diag_down, diag_up],
            [at(0, 2), at(1, -1), at(1, 1)],
            gain,
            wq,
            wkv,
            total,
            waits,
            b,
        )

    total0 = second(0, [vmem(low_rows)])
    low_rows, high_rows, far_rows = up(low_rows), down(high_rows), across(far_rows)
    far_second, cache_other = cut_out(
        [(far, 1, 0, rows), (hbm(caches), None, 0, 0)],
        [vmem(low_rows), vmem(high_rows), hbm(total0[0])],
    )
    cache_sent = cache_other
    cache_other, far_second = mate(cache_other), across(far_second)

    def ready(b, last, total, waits):
        q, kv, send = finish_products(
            spots, b, last, at(1, 2), gain, wq, wkv, total, qb, kvb, cosine, sine, waits
        )
        return q, kv, mate(send)

    def attend(b, q, kv, other, waits):
        return attention(
            spots, b, q, kv, other, caches, cache_other, cosine, sine, waits
        )

    def begin(attended, first_rows):
        parts = [first_rows, rows - first_rows]
        return project(spots, attended, wo, [at(1, 2)], [parts], send=True)

    def next_three(attended, waits):
        targets = [at(0, 2), at(1, 1), at(1, -1)]
        return project(spots, attended, wo, targets, [[rows]] * 3, waits)

    def last_four(attended, waits):
        targets = [at(0, -1), at(0, 1), at(1, 0), at(0, 0)]
        return project(spots, attended, wo, targets, [[rows]] * 4, waits)

    def fan(a, b, c):
        return down(a), up(b), across(c)

    q0, kv0, other0 = ready(0, [low_rows, high_rows, far_rows], total0, [vmem(cache_sent)])
    total1 = second(1, [vmem(kv0)])
    attended0, pages0 = attend(0, q0, kv0, other0, [hbm(total1[0])])
    low, high = begin(attended0, cut)
    q1, kv1, other1 = ready(1, [far_second], total1, [vmem(low)])
    low, high = down(low), up(high)
    a_, b_, c_ = next_three(attended0, [vmem(kv1)])
    a_ = down(a_)
    b_, c_ = add_up(
        [
            [(b_, 0, HERE), (high, cut, LINK)],
            [(c_, 0, HERE), (low, 0, LINK)],
        ],
        [vmem(other1)],
    )
    d_, e_, g_, own0 = last_four(attended0, [vmem(c_)])
    e_ = up(e_)
    b_, c_ = up(b_), across(c_)
    attended1, pages1 = attend(1, q1, kv1, other1, [hbm(own0)])
    me_there = lax.axis_index("segment").astype(jnp.int32)
    page = pages0.shape[1:]
    all_slots, half_slots = (sections,) + page, (sections // 2,) + page
    pages_each = pages0.shape[0]
    bits = [me_there // 2**k % 2 for k in range(4)]

    def first_trade(scalar_ref, ins, outs):
        slots, sent = outs
        for o in range(sections):
            slots[o] = jnp.zeros(page, BF)
        for p in range(blocks * pages_each):
            slots[scalar_ref[1 + p]] = ins[p // pages_each][p % pages_each]
        pick_sent(scalar_ref[0], slots, sent, 0, sections)

    def later_trade(before, step):
        def run(scalar_ref, ins, outs):
            merge_got(scalar_ref[0], ins[0], ins[1], outs[0], before, sections)
            pick_sent(scalar_ref[1], outs[0], outs[1], step, sections)

        return run

    def last_trade(scalar_ref, ins, outs):
        merge_got(scalar_ref[0], ins[0], ins[1], outs[0], 3, sections)

    def trade_with(sent, step):
        return lax.ppermute(sent, "segment", [(i, i ^ 1 << step) for i in range(sections)])

    fewer = rows // 3
    low1, high1 = begin(attended1, fewer)
    trade = Trade(
        jnp.concatenate([bits[0][None], page_owner[0]]),
        [hbm(pages0), hbm(pages1)],
        [all_slots, half_slots],
        first_trade,
    )
    d_, g_, slots, sent = add_up(
        [[(d_, 0, HERE), (a_, 0, LINK), (c_, 0, LINK)], [(g_, 0, HERE), (b_, 0, LINK)]],
        [vmem(low1)],
        trade,
    )
    low1, high1 = down(low1), up(high1)
    d_, g_ = down(d_), across(g_)
    got = trade_with(sent, 0)
    a1, b1, c1 = next_three(attended1, [vmem(e_)])
    trade = Trade(
        jnp.stack([bits[0], bits[2]]),
        [hbm(slots), got],
        [all_slots, half_slots],
        later_trade(0, 2),
    )
    a1, b1, c1, done0, slots, sent = add_up(
        [
            [(a1, 0, HERE)],
            [(b1, 0, HERE), (high1, fewer, LOOSE)],
            [(c1, 0, HERE), (low1, 0, LOOSE)],
            [(rows_all, 0, 0), (own0, 0, HERE), (e_, 0, LINK), (d_, 0, LINK), (g_, 0, LINK)],
        ],
        (),
        trade,
    )
    a1, b1, c1 = fan(a1, b1, c1)
    first = lax.ppermute(done0, "segment", onward)
    got = trade_with(sent, 2)
    d1, e1, g1, own1 = last_four(attended1, [got])
    e1 = up(e1)
    (next_hidden,) = put_block(None, [first], place, blocks)
    slots, sent = trade_alone(
        Trade(
            jnp.stack([bits[2], bits[1]]),
            [hbm(slots), got],
            [all_slots, half_slots],
            later_trade(2, 1),
        ),
        [hbm(own1)],
    )
    d1, g1 = add_up(
        [[(d1, 0, HERE), (a1, 0, LINK), (c1, 0, LINK)], [(g1, 0, HERE), (b1, 0, LINK)]],
        [hbm(next_hidden), hbm(sent)],
    )
    d1, g1 = down(d1), across(g1)
    got = trade_with(sent, 1)
    done1 = add_up(
        [[(rows_all, 0, 1), (own1, 0, HERE), (e1, 0, LINK), (d1, 0, LINK), (g1, 0, LINK)]], [got]
    )
    last = [lax.ppermute(part, "segment", onward) for part in done1]
    slots, sent = trade_alone(
        Trade(
            jnp.stack([bits[1], bits[3]]),
            [hbm(slots), got],
            [all_slots, half_slots],
            later_trade(1, 3),
        ),
        [vmem(done1[0])],
    )
    got = trade_with(sent, 3)
    (shipped,) = trade_alone(Trade(bits[3][None], [hbm(slots), got], [all_slots], last_trade), ())
    (next_hidden,) = put_block(next_hidden, last, 1 - place, blocks)
    return next_hidden[None], jnp.swapaxes(shipped, 2, 3)[None]


def solution(mesh):
    return jax.shard_map(
        local,
        mesh=mesh,
        in_specs=(
            P("segment", None, None, "tensor"),
            P("segment", None),
            P("segment", None, "tensor"),
            P("segment", "tensor"),
            P("segment", None, None, "tensor"),
            P("segment", None, "tensor"),
            P("segment", "tensor", None),
            P("segment", None, None, None, "tensor"),
            P("segment", None),
            P("segment", None),
            P("segment", None),
        ),
        out_specs=(P("segment", None, None, "tensor"), P("segment", None, None, None, "tensor")),
        check_vma=False,
    )
```
